32 devices in a mesh: expert: 16 (over z, y, core), tensor: 2 (over x).
Axes of the slice: x: 2, y: 2, z: 4, core: 2. Of those that a mesh axis runs over, the one named last changes fastest.
Arguments:
- tokens: bfloat16 [2048, 2048], P('expert', 'tensor'), may hold values from -6 to 6
- grad_out: bfloat16 [2048, 2048], P('expert', 'tensor'), may hold values from -6 to 6
- gates: float32 [2048, 6], P('expert'), may hold values from 0.1 to 1
- expert_ids: int32 [2048, 6], P('expert'), may hold values from 0 to 15, all different within a row; in each aligned block of 128 rows (0 to 127, 128 to 255, ...) at most 64 rows name the same one
- w_gate: bfloat16 [16, 2048, 1408], P('expert', None, 'tensor'), may hold values from -0.125 to 0.125
- w_up: bfloat16 [16, 2048, 1408], P('expert', None, 'tensor'), may hold values from -0.125 to 0.125
- w_down: bfloat16 [16, 1408, 2048], P('expert', 'tensor'), may hold values from -0.15625 to 0.15625
Outputs:
- mixed: bfloat16 [2048, 2048], P('expert', 'tensor')
- grad_tokens: bfloat16 [2048, 2048], P('expert', 'tensor')
- grad_gates: float32 [2048, 6], P('expert')
- grad_w_gate: bfloat16 [16, 2048, 1408], P('expert', None, 'tensor')
- grad_w_up: bfloat16 [16, 2048, 1408], P('expert', None, 'tensor')
- grad_w_down: bfloat16 [16, 1408, 2048], P('expert', 'tensor')
The draws below stay inside these ranges and needn't reach their ends.
Inputs may be any that keep to these rules, and one draw needn't show every extreme that they name: `expert_ids`: each row names 6 different experts. In each aligned block of 128 rows (the tokens of one index of expert) no expert is named by more than 64 rows, and some block names some expert exactly 64 times.
All inputs are finite; a program needn't handle non-finite values.
Results may differ from the reference program's by a relative error of at most 0.0064.
Values may be sent and summed in bfloat16 or wider, within the bound.
No kernel may reach another device: no remote copies, remote signals or barrier semaphores. Data moves between devices by JAX's collectives and lax.ppermute only.
A program may use at most 128 MiB of HBM per device.

```python
import math
import jax
import jax.numpy as jnp
import numpy as np
from jax import lax

D = 2048
FF = 1408
TOP = 6
TOK_DEV = 128
EXPERTS = 16
TOKENS = 2048
CAP = 64
EXPERT_ROWS = 1024


def block_scale(stream_key, extent, cuts, smallest, high):
    level, own = 1.0, jax.random.fold_in(stream_key, 6)
    for dim, shards_of in cuts:
        heights = jnp.exp(jax.random.uniform(jax.random.fold_in(own, dim), (shards_of,), jnp.float32, smallest / len(cuts), high / len(cuts)))
        level = level * jnp.repeat(heights, extent[dim] // shards_of).reshape([-1 if axis == dim else 1 for axis in range(len(extent))])
    return level


def deal_out(rng, own, number, rows, count, top, reach, slope):
    ranking = jax.random.permutation(rng, count)
    packed, usual = shares(count, rows * top, reach, slope, True), shares(count, rows * top, reach, slope, False)
    places = jnp.arange(count)

    def named(sizes, offset_by):
        used = int((sizes > 0).sum())
        fixed = max(1, used // 4)
        moved = fixed + (places - fixed + offset_by * (used - fixed)) % max(1, count - fixed)
        return jnp.zeros((count,), jnp.int32).at[ranking[jnp.where(places < fixed, places, moved)]].set(jnp.asarray(sizes, jnp.int32))

    sizes = jnp.where(number % 4 == 0, named(packed, number // 4), named(usual, number - number // 4 - 1))
    mixed = jax.random.permutation(jax.random.fold_in(own, 3), count)
    giver, sink = mixed[0:count // 2 * 2:2], mixed[1:count // 2 * 2:2]
    room = jnp.minimum(sizes[giver] - 1, reach - sizes[sink]) // 2
    room = jnp.where((giver == ranking[0]) | (sink == ranking[0]) | (sizes[sink] == 0), 0, jnp.maximum(room, 0))
    moved = jax.random.randint(jax.random.fold_in(own, 4), (count // 2,), 0, 1 << 20) % (room + 1)
    sizes = sizes.at[giver].add(-moved).at[sink].add(moved)
    items = jnp.searchsorted(jnp.cumsum(sizes), jnp.arange(rows * top), side="right").astype(jnp.int32)
    table = items.reshape(top, rows).T
    table = table[jax.random.permutation(jax.random.fold_in(own, 1), rows)]
    offset_by = jax.random.randint(jax.random.fold_in(own, 2), (rows, 1), 0, top)
    return jnp.take_along_axis(table, (jnp.arange(top)[None, :] + offset_by) % top, axis=1)


def shares(amount, total, limit, skew, full):
    loads = [(1 << 20) // math.isqrt(rank ** skew) + 1 for rank in range(1, amount + 1)]
    largest = limit if full else min(limit, max(-(-total // amount), total * loads[0] // sum(loads)))
    least = 1 if total - largest >= amount - 1 else 0
    holding, spare = [largest] + [least] * (amount - 1), total - largest - least * (amount - 1)
    while spare > 0:
        free = [i for i in range(1, amount) if holding[i] < largest] or [i for i in range(1, amount) if holding[i] < limit]
        mass, left = sum([loads[i] for i in free]), spare
        for i in free:
            more = min(limit - holding[i], max(1, left * loads[i] // mass), spare)
            holding[i] = holding[i] + more
            spare = spare - more
    return np.array(holding)


def bell_draw(rng, dims, deviation, bound, shards=(), kind=jnp.bfloat16):
    result = jax.random.normal(rng, dims, jnp.float32) * deviation
    if len(shards) > 0:
        result = block_scale(rng, dims, shards, -0.22, 0.18) * result
    return jnp.clip(result, min=-bound, max=bound).astype(kind)


def setup_inputs(seed: int = 0) -> dict:
    seeds = jax.random.split(jax.random.key(seed), 8)
    tokens = bell_draw(seeds[0], (TOKENS, D), 1.0, 6.0, ((0, 16), (1, 2)))
    grad_out = bell_draw(seeds[1], (TOKENS, D), 1.0, 6.0, ((0, 16), (1, 2)))
    gates = jnp.clip(jnp.exp(math.log(1.0) - 2.3025851 * jax.random.uniform(seeds[2], (TOKENS, TOP), jnp.float32) ** block_scale(seeds[2], (TOKENS, TOP), ((0, 16),), -0.2, 0.2)), 0.1, 1.0)
    expert_ids_keys = jax.random.split(jax.random.fold_in(seeds[3], 1), TOKENS // TOK_DEV)
    expert_ids_turns = jax.random.permutation(jax.random.fold_in(seeds[3], 3), TOKENS // TOK_DEV)
    expert_ids = jax.vmap(lambda own, number: deal_out(jax.random.fold_in(seeds[3], 2), own, number, TOK_DEV, EXPERTS, TOP, CAP, 1))(expert_ids_keys, expert_ids_turns).reshape((TOKENS, TOP))
    w_gate = bell_draw(seeds[4], (EXPERTS, D, FF), D ** -0.5, 0.125, ((0, 16), (2, 2)))
    w_up = bell_draw(seeds[5], (EXPERTS, D, FF), D ** -0.5, 0.125, ((0, 16), (2, 2)))
    w_down = bell_draw(seeds[6], (EXPERTS, FF, D), FF ** -0.5, 0.15625, ((0, 16), (1, 2)))
    return dict(tokens=tokens, grad_out=grad_out, gates=gates, expert_ids=expert_ids, w_gate=w_gate, w_up=w_up, w_down=w_down)


def expert_pass(rows, grad_rows, weight_gate, weight_up, weight_down):
    gate_pre = jnp.dot(rows, weight_gate, preferred_element_type=jnp.float32)
    up_pre = jnp.dot(rows, weight_up, preferred_element_type=jnp.float32)
    sig = jax.nn.sigmoid(gate_pre)
    act = (gate_pre * sig * up_pre).astype(jnp.bfloat16)
    expert_out = jnp.dot(act, weight_down, preferred_element_type=jnp.float32).astype(jnp.bfloat16)
    grad_act = jnp.dot(grad_rows, weight_down.T, preferred_element_type=jnp.float32)
    grad_gate_pre = (grad_act * up_pre * sig * (1.0 + gate_pre * (1.0 - sig))).astype(jnp.bfloat16)
    grad_up_pre = (grad_act * gate_pre * sig).astype(jnp.bfloat16)
    grad_down = jnp.dot(act.T, grad_rows, preferred_element_type=jnp.float32).astype(jnp.bfloat16)
    grad_gate = jnp.dot(rows.T, grad_gate_pre, preferred_element_type=jnp.float32).astype(jnp.bfloat16)
    grad_up = jnp.dot(rows.T, grad_up_pre, preferred_element_type=jnp.float32).astype(jnp.bfloat16)
    grad_x = (jnp.dot(grad_gate_pre, weight_gate.T, preferred_element_type=jnp.float32)
              + jnp.dot(grad_up_pre, weight_up.T, preferred_element_type=jnp.float32)).astype(jnp.bfloat16)
    return expert_out, grad_x, grad_gate, grad_up, grad_down


def reference(tokens, grad_out, gates, expert_ids, w_gate, w_up, w_down):
    pair_total = TOKENS * TOP
    flat_ids = expert_ids.reshape(-1)
    pair_token = (jnp.arange(pair_total, dtype=jnp.int32) // TOP).astype(jnp.int32)
    scaled = (gates.reshape(-1)[:, None] * grad_out[pair_token].astype(jnp.float32)).astype(grad_out.dtype)
    tokens_pad = jnp.concatenate([tokens, jnp.zeros((1, D), tokens.dtype)], axis=0)
    scaled_pad = jnp.concatenate([scaled, jnp.zeros((1, D), scaled.dtype)], axis=0)

    def one_expert(operands):
        expert_index, weight_gate, weight_up, weight_down = operands
        chosen = jnp.nonzero(flat_ids == expert_index, size=EXPERT_ROWS, fill_value=pair_total)[0].astype(jnp.int32)
        rows = tokens_pad[(chosen // TOP).astype(jnp.int32)]
        grad_rows = scaled_pad[chosen]
        results = expert_pass(rows, grad_rows, weight_gate, weight_up, weight_down)
        return results + (chosen,)

    expert_out, grad_x, grad_gate, grad_up, grad_down, chosen = lax.map(
        one_expert, (jnp.arange(EXPERTS, dtype=jnp.int32), w_gate, w_up, w_down))
    chosen = chosen.reshape(-1)
    out_pairs = jnp.zeros((pair_total + 1, D), expert_out.dtype).at[chosen].set(expert_out.reshape(-1, D))[:pair_total]
    dx_pairs = jnp.zeros((pair_total + 1, D), grad_x.dtype).at[chosen].set(grad_x.reshape(-1, D))[:pair_total]
    out_pairs = out_pairs.reshape(TOKENS, TOP, D).astype(jnp.float32)
    dx_pairs = dx_pairs.reshape(TOKENS, TOP, D).astype(jnp.float32)
    mixed = jnp.sum(gates[:, :, None] * out_pairs, axis=1).astype(tokens.dtype)
    grad_gates = jnp.sum(grad_out.astype(jnp.float32)[:, None, :] * out_pairs, axis=2)
    grad_tokens = jnp.sum(dx_pairs, axis=1).astype(tokens.dtype)
    return (mixed, grad_tokens, grad_gates, grad_gate, grad_up, grad_down)
```

```python
import jax
import jax.numpy as jnp
from jax import lax
from jax.sharding import PartitionSpec as P

F32 = jnp.float32
BF16 = jnp.bfloat16


def slots_body(tokens, grad_out, gates, expert_ids, w_gate, w_up, w_down):
    expert_count = lax.axis_size("expert")
    tok_count = expert_ids.shape[0]
    top_count = expert_ids.shape[1]
    capacity = tok_count * top_count * 4 // (3 * expert_count)
    slot_total = expert_count * capacity
    flat_ids = expert_ids.reshape(-1)
    member = (flat_ids[:, None] == jnp.arange(expert_count, dtype=jnp.int32)[None, :]).astype(
        jnp.int32
    )
    earlier = jnp.cumsum(member, axis=0) - member
    position = jnp.sum(earlier * member, axis=1)
    slot_index = flat_ids * capacity + position
    pair_token = jnp.arange(tok_count * top_count, dtype=jnp.int32) // top_count
    pair_gate = gates.reshape(-1)[:, None]

    def pack(rows, scaled):
        picked = rows[pair_token]
        if scaled:
            picked = (pair_gate * picked.astype(jnp.float32)).astype(jnp.bfloat16)
        buffer = jnp.zeros((slot_total, rows.shape[1]), jnp.bfloat16).at[slot_index].set(picked)
        return buffer.reshape(expert_count, capacity, rows.shape[1])

    def dispatch(rows, scaled):
        arrived = lax.all_to_all(
            pack(rows, scaled), "expert", split_axis=0, concat_axis=0, tiled=True
        )
        arrived = arrived.reshape(slot_total, rows.shape[1])
        return lax.all_gather(arrived, "tensor", axis=1, tiled=True)

    def give_back(partial_value):
        shares = lax.psum_scatter(partial_value, "tensor", scatter_dimension=1, tiled=True).astype(
            jnp.bfloat16
        )
        width = shares.shape[1]
        shares = shares.reshape(expert_count, capacity, width)
        returned = lax.all_to_all(shares, "expert", split_axis=0, concat_axis=0, tiled=True)
        return returned.reshape(slot_total, width)[slot_index].reshape(tok_count, top_count, width)

    weight_gate = w_gate[0]
    weight_up = w_up[0]
    weight_down = w_down[0]
    full_rows = dispatch(tokens, False)
    gate_pre = jnp.dot(full_rows, weight_gate, preferred_element_type=jnp.float32)
    up_pre = jnp.dot(full_rows, weight_up, preferred_element_type=jnp.float32)
    sig = jax.nn.sigmoid(gate_pre)
    act = (gate_pre * sig * up_pre).astype(jnp.bfloat16)
    outputs = give_back(jnp.dot(act, weight_down, preferred_element_type=jnp.float32)).astype(
        jnp.float32
    )
    mixed = jnp.sum(gates[:, :, None] * outputs, axis=1).astype(jnp.bfloat16)
    gate_terms = jnp.sum(grad_out.astype(jnp.float32)[:, None, :] * outputs, axis=2)
    grad_gates = lax.psum(gate_terms, "tensor")
    grad_rows = dispatch(grad_out, True)
    contract_last = (((1,), (1,)), ((), ()))
    contract_first = (((0,), (0,)), ((), ()))
    grad_act = lax.dot_general(
        grad_rows, weight_down, contract_last, preferred_element_type=jnp.float32
    )
    grad_gate_pre = (grad_act * up_pre * sig * (1.0 + gate_pre * (1.0 - sig))).astype(jnp.bfloat16)
    grad_up_pre = (grad_act * gate_pre * sig).astype(jnp.bfloat16)
    grad_down = lax.dot_general(
        act, grad_rows, contract_first, preferred_element_type=jnp.float32
    ).astype(jnp.bfloat16)
    grad_gate = lax.dot_general(
        full_rows, grad_gate_pre, contract_first, preferred_element_type=jnp.float32
    ).astype(jnp.bfloat16)
    grad_up = lax.dot_general(
        full_rows, grad_up_pre, contract_first, preferred_element_type=jnp.float32
    ).astype(jnp.bfloat16)
    input_terms = lax.dot_general(
        grad_gate_pre, weight_gate, contract_last, preferred_element_type=jnp.float32
    ) + lax.dot_general(grad_up_pre, weight_up, contract_last, preferred_element_type=jnp.float32)
    input_pairs = give_back(input_terms).astype(jnp.float32)
    grad_tokens = jnp.sum(input_pairs, axis=1).astype(jnp.bfloat16)
    return (mixed, grad_tokens, grad_gates, grad_gate[None], grad_up[None], grad_down[None])


def after(value, *others):
    return lax.optimization_barrier((value, *others))[0]


def gather_body(tokens, grad_out, gates, expert_ids, w_gate, w_up, w_down):
    expert_count = lax.axis_size("expert")
    tok_count, top_count = expert_ids.shape
    capacity = tok_count * top_count * 4 // (3 * expert_count)
    width = tokens.shape[1]
    half = width // 2
    column = expert_count // 4
    me = lax.axis_index("expert")
    side = lax.axis_index("tensor")

    core_pairs = [(e, e ^ 1) for e in range(expert_count)]
    chip_pairs = [(e, e ^ 2) for e in range(expert_count)]

    def swap_core(value):
        return lax.ppermute(value, "expert", core_pairs)

    def swap_pair(value):
        return lax.ppermute(value, "expert", chip_pairs)

    def swap_side(value):
        return lax.ppermute(value, "tensor", [(0, 1), (1, 0)])

    def shift(value, step):
        return lax.ppermute(
            value, "expert", [(e, (e + 4 * step) % expert_count) for e in range(expert_count)]
        )

    rel_core, rel_pair, rel_step = jnp.meshgrid(
        jnp.arange(2), jnp.arange(2), jnp.arange(column), indexing="ij"
    )
    block_of = (
        ((me // 4 - rel_step) % column) * 4 + (((me // 2) % 2) ^ rel_pair) * 2 + ((me % 2) ^ rel_core)
    ).reshape(-1)

    routing = jnp.concatenate([expert_ids.astype(F32), gates], axis=1)
    routing = lax.all_gather(routing, "expert")[block_of]
    named = routing[:, :, :top_count] == me.astype(F32)
    gate_of_token = jnp.sum(jnp.where(named, routing[:, :, top_count:], 0.0), axis=2)
    member = jnp.any(named, axis=2).astype(jnp.int32)
    position = jnp.where(member > 0, jnp.cumsum(member, axis=1) - 1, -1)
    pick = position[:, None, :] == jnp.arange(capacity, dtype=jnp.int32)[None, :, None]
    gate_row = jnp.sum(jnp.where(pick, gate_of_token[:, None, :], 0.0), axis=2).reshape(-1, 1)
    pick_bf = pick.astype(BF16)

    def spread(rows, start):
        own = after(jnp.stack([rows[:, :half], rows[:, half:]]), *start)
        parts = [own] + [shift(own, step) for step in range(1, column)]
        a = jnp.stack([part[0] for part in parts])
        b = jnp.stack([part[1] for part in parts])
        a = jnp.stack([a, swap_side(a)], axis=1)
        b = jnp.stack([b, swap_pair(b)])
        a = jnp.stack([a, swap_pair(a)])
        b = jnp.stack([b, swap_side(b)], axis=2)
        return (a, swap_core(a)), (b, swap_core(b)), parts

    def pick_rows(a, b):
        halves = []
        for piece in (a, b):
            blocks = jnp.stack(piece).reshape(4 * column, 2, tok_count, half)
            halves.append(
                jnp.einsum("bst,bxth->bsxh", pick_bf, blocks, preferred_element_type=F32).astype(BF16)
            )
        rows = jnp.concatenate(halves, axis=3)
        rows = jnp.where(side == 0, rows, rows[:, :, ::-1])
        return rows.reshape(-1, 2 * width)

    def put_back(values):
        values = values.astype(BF16).reshape(4 * column, capacity, 2, width)
        values = jnp.where(side == 0, values, values[:, :, ::-1])
        blocks = jnp.einsum("bst,bsxh->bxth", pick_bf, values, preferred_element_type=F32)
        return blocks.astype(BF16).reshape(2, 2, column, 2, tok_count, width)

    def add(mine, theirs):
        return (mine.astype(F32) + theirs.astype(F32)).astype(BF16)

    def collect(blocks):
        halves = blocks[..., :half], blocks[..., half:]
        a, b = (add(piece[0], swap_core(piece[1])) for piece in halves)
        a = add(a[0], swap_pair(a[1]))
        b = add(b[:, :, 0], swap_side(b[:, :, 1]))
        a = add(a[:, 0], swap_side(a[:, 1]))
        b = add(b[0], swap_pair(b[1]))
        both = jnp.stack([a, b], axis=1)
        total = both[0].astype(F32)
        for step in range(1, column):
            total = total + shift(both[step], column - step).astype(F32)
        return jnp.concatenate([total[0], total[1]], axis=1).astype(BF16)

    weight_gate, weight_up, weight_down = w_gate[0], w_up[0], w_down[0]
    contract_last = (((1,), (1,)), ((), ()))
    contract_first = (((0,), (0,)), ((), ()))

    token_a, token_b, token_parts = spread(tokens, ())
    grad_a, grad_b, _ = spread(grad_out, token_parts)

    full_rows = pick_rows(token_a, token_b)
    gate_pre = jnp.dot(full_rows, weight_gate, preferred_element_type=F32)
    up_pre = jnp.dot(full_rows, weight_up, preferred_element_type=F32)
    sig = jax.nn.sigmoid(gate_pre)
    act = gate_pre * sig * up_pre
    scaled_act = (gate_row * act).astype(BF16)
    mixed = collect(put_back(jnp.dot(scaled_act, weight_down, preferred_element_type=F32)))

    grad_rows = pick_rows(grad_a, grad_b)
    plain = lax.dot_general(grad_rows, weight_down, contract_last, preferred_element_type=F32)
    gate_sums = jnp.sum(act * plain, axis=1)
    grad_act = gate_row * plain
    grad_gate_pre = (grad_act * up_pre * sig * (1.0 + gate_pre * (1.0 - sig))).astype(BF16)
    grad_up_pre = (grad_act * gate_pre * sig).astype(BF16)
    input_terms = lax.dot_general(
        grad_gate_pre, weight_gate, contract_last, preferred_element_type=F32
    ) + lax.dot_general(grad_up_pre, weight_up, contract_last, preferred_element_type=F32)
    grad_tokens = collect(put_back(input_terms))

    token_sums = jnp.sum(
        jnp.where(pick, gate_sums.reshape(4 * column, capacity, 1), 0.0), axis=1
    )
    token_sums = token_sums + swap_side(token_sums)
    token_sums = jnp.zeros_like(token_sums).at[block_of].set(token_sums)
    expert_sums = lax.all_to_all(token_sums, "expert", split_axis=0, concat_axis=0, tiled=True)
    chosen = expert_ids[None] == jnp.arange(expert_count, dtype=jnp.int32)[:, None, None]
    grad_gates = jnp.sum(jnp.where(chosen, expert_sums[:, :, None], 0.0), axis=0)

    def weight_grad(left, right):
        return lax.dot_general(left, right, contract_first, preferred_element_type=F32).astype(BF16)[None]

    grad_down = weight_grad(scaled_act, grad_rows)
    grad_gate = weight_grad(full_rows, grad_gate_pre)
    grad_up = weight_grad(full_rows, grad_up_pre)
    return (mixed, grad_tokens, grad_gates, grad_gate, grad_up, grad_down)


def body(tokens, grad_out, gates, expert_ids, w_gate, w_up, w_down):
    expert_count = lax.axis_size("expert")
    tok_count, top_count = expert_ids.shape
    slot_total = tok_count * top_count * 4 // (3 * expert_count) * expert_count
    gathers = expert_count * tok_count <= 2 * slot_total
    shaped = lax.axis_size("tensor") == 2 and expert_count % 4 == 0
    plan = gather_body if gathers and shaped else slots_body
    return plan(tokens, grad_out, gates, expert_ids, w_gate, w_up, w_down)


def solution(mesh):
    placed = (
        P("expert", "tensor"),
        P("expert", "tensor"),
        P("expert", None),
        P("expert", None),
        P("expert", None, "tensor"),
        P("expert", None, "tensor"),
        P("expert", "tensor", None),
    )
    return jax.shard_map(
        body,
        mesh=mesh,
        in_specs=placed,
        out_specs=(
            P("expert", "tensor"),
            P("expert", "tensor"),
            P("expert", None),
            P("expert", None, "tensor"),
            P("expert", None, "tensor"),
            P("expert", "tensor", None),
        ),
        check_vma=False,
    )
```

```python
import functools

import jax
import jax.numpy as jnp
from jax import lax
from jax.experimental import pallas as pl
from jax.experimental.pallas import tpu as pltpu
from jax.sharding import PartitionSpec as P

F32 = jnp.float32
BF16 = jnp.bfloat16


def slots_body(tokens, grad_out, gates, expert_ids, w_gate, w_up, w_down):
    expert_count = lax.axis_size("expert")
    tok_count = expert_ids.shape[0]
    top_count = expert_ids.shape[1]
    capacity = tok_count * top_count * 4 // (3 * expert_count)
    slot_total = expert_count * capacity
    flat_ids = expert_ids.reshape(-1)
    member = (flat_ids[:, None] == jnp.arange(expert_count, dtype=jnp.int32)[None, :]).astype(
        jnp.int32
    )
    earlier = jnp.cumsum(member, axis=0) - member
    position = jnp.sum(earlier * member, axis=1)
    slot_index = flat_ids * capacity + position
    pair_token = jnp.arange(tok_count * top_count, dtype=jnp.int32) // top_count
    pair_gate = gates.reshape(-1)[:, None]

    def pack(rows, scaled):
        picked = rows[pair_token]
        if scaled:
            picked = (pair_gate * picked.astype(jnp.float32)).astype(jnp.bfloat16)
        buffer = jnp.zeros((slot_total, rows.shape[1]), jnp.bfloat16).at[slot_index].set(picked)
        return buffer.reshape(expert_count, capacity, rows.shape[1])

    def dispatch(rows, scaled):
        arrived = lax.all_to_all(
            pack(rows, scaled), "expert", split_axis=0, concat_axis=0, tiled=True
        )
        arrived = arrived.reshape(slot_total, rows.shape[1])
        return lax.all_gather(arrived, "tensor", axis=1, tiled=True)

    def give_back(partial_value):
        shares = lax.psum_scatter(partial_value, "tensor", scatter_dimension=1, tiled=True).astype(
            jnp.bfloat16
        )
        width = shares.shape[1]
        shares = shares.reshape(expert_count, capacity, width)
        returned = lax.all_to_all(shares, "expert", split_axis=0, concat_axis=0, tiled=True)
        return returned.reshape(slot_total, width)[slot_index].reshape(tok_count, top_count, width)

    weight_gate = w_gate[0]
    weight_up = w_up[0]
    weight_down = w_down[0]
    full_rows = dispatch(tokens, False)
    gate_pre = jnp.dot(full_rows, weight_gate, preferred_element_type=jnp.float32)
    up_pre = jnp.dot(full_rows, weight_up, preferred_element_type=jnp.float32)
    sig = jax.nn.sigmoid(gate_pre)
    act = (gate_pre * sig * up_pre).astype(jnp.bfloat16)
    outputs = give_back(jnp.dot(act, weight_down, preferred_element_type=jnp.float32)).astype(
        jnp.float32
    )
    mixed = jnp.sum(gates[:, :, None] * outputs, axis=1).astype(jnp.bfloat16)
    gate_terms = jnp.sum(grad_out.astype(jnp.float32)[:, None, :] * outputs, axis=2)
    grad_gates = lax.psum(gate_terms, "tensor")
    grad_rows = dispatch(grad_out, True)
    contract_last = (((1,), (1,)), ((), ()))
    contract_first = (((0,), (0,)), ((), ()))
    grad_act = lax.dot_general(
        grad_rows, weight_down, contract_last, preferred_element_type=jnp.float32
    )
    grad_gate_pre = (grad_act * up_pre * sig * (1.0 + gate_pre * (1.0 - sig))).astype(jnp.bfloat16)
    grad_up_pre = (grad_act * gate_pre * sig).astype(jnp.bfloat16)
    grad_down = lax.dot_general(
        act, grad_rows, contract_first, preferred_element_type=jnp.float32
    ).astype(jnp.bfloat16)
    grad_gate = lax.dot_general(
        full_rows, grad_gate_pre, contract_first, preferred_element_type=jnp.float32
    ).astype(jnp.bfloat16)
    grad_up = lax.dot_general(
        full_rows, grad_up_pre, contract_first, preferred_element_type=jnp.float32
    ).astype(jnp.bfloat16)
    input_terms = lax.dot_general(
        grad_gate_pre, weight_gate, contract_last, preferred_element_type=jnp.float32
    ) + lax.dot_general(grad_up_pre, weight_up, contract_last, preferred_element_type=jnp.float32)
    input_pairs = give_back(input_terms).astype(jnp.float32)
    grad_tokens = jnp.sum(input_pairs, axis=1).astype(jnp.bfloat16)
    return (mixed, grad_tokens, grad_gates, grad_gate[None], grad_up[None], grad_down[None])


LAST = (((1,), (1,)), ((), ()))
FIRST = (((0,), (0,)), ((), ()))


def dot(left, right, dims=(((1,), (0,)), ((), ()))):
    return lax.dot_general(left, right, dims, preferred_element_type=F32)


def after(value, *others):
    return lax.optimization_barrier((value, *others))[0]


def picks(pos, place, capacity):
    row = pos[0, place : place + 1, :]
    slot = lax.broadcasted_iota(jnp.int32, (capacity, row.shape[1]), 0).astype(F32)
    return row == slot


def gather_rows(side, pos, pieces, rows, capacity):
    half = pieces[0].shape[-1]
    for core in range(2):
        for pair in range(2):
            place = 2 * core + pair
            pick = picks(pos, place, capacity).astype(BF16)
            at = pl.ds(place * capacity, capacity)
            for far in range(2):
                column = pl.multiple_of((side ^ far) * 2 * half, half)
                a = pieces[2 * core + pair][far, 0]
                b = pieces[4 + 2 * core + far][pair, 0]
                rows[at, pl.ds(column, half)] = dot(pick, a).astype(BF16)
                rows[at, pl.ds(column + half, half)] = dot(pick, b).astype(BF16)


def gate_rows(pos, gate, capacity):
    out = []
    for place in range(4):
        pick = picks(pos, place, capacity)
        out.append(jnp.sum(jnp.where(pick, gate[0, place : place + 1, :], 0.0), axis=1, keepdims=True))
    return jnp.concatenate(out, axis=0)


def scatter_rows(side, pos, values, outs, capacity):
    half = outs[0].shape[-1]
    for core in range(2):
        for pair in range(2):
            place = 2 * core + pair
            pick = picks(pos, place, capacity).astype(BF16)
            at = pl.ds(place * capacity, capacity)
            for far in range(2):
                column = pl.multiple_of((side ^ far) * 2 * half, half)
                a = dot(pick, values[at, pl.ds(column, half)], FIRST)
                outs[core][pair, far, 0] = a.astype(BF16)
                b = dot(pick, values[at, pl.ds(column + half, half)], FIRST)
                outs[2 + core][far, pair, 0] = b.astype(BF16)


def up_kernel(capacity, side, pos, gate, *refs):
    pieces, (weight_gate, weight_up, rows, gate_pre, up_pre, scaled) = refs[:8], refs[8:]
    gather_rows(side[0], pos, pieces, rows, capacity)
    gates = gate_rows(pos, gate, capacity)
    got = rows[...]
    pre = dot(got, weight_gate[...])
    up = dot(got, weight_up[...])
    gate_pre[...] = pre
    up_pre[...] = up
    scaled[...] = (gates * (pre * jax.nn.sigmoid(pre) * up)).astype(BF16)


def mix_kernel(capacity, side, pos, scaled, weight_down, *refs):
    outs, values = refs[:4], refs[4]
    values[...] = dot(scaled[...], weight_down[...]).astype(BF16)
    scatter_rows(side[0], pos, values, outs, capacity)


def back_kernel(capacity, side, pos, gate, *refs):
    pieces, (weight_down, gate_pre, up_pre, rows, grad_gate_pre, grad_up_pre, sums) = refs[:8], refs[8:]
    gather_rows(side[0], pos, pieces, rows, capacity)
    gates = gate_rows(pos, gate, capacity)
    plain = dot(rows[...], weight_down[...], LAST)
    pre, up = gate_pre[...], up_pre[...]
    sig = jax.nn.sigmoid(pre)
    silu = pre * sig
    row_sums = jnp.sum(silu * up * plain, axis=1, keepdims=True)
    grad_act = gates * plain
    grad_gate_pre[...] = (grad_act * up * sig * (1.0 + pre * (1.0 - sig))).astype(BF16)
    grad_up_pre[...] = (grad_act * silu).astype(BF16)
    for place in range(4):
        pick = picks(pos, place, capacity)
        own = row_sums[place * capacity : (place + 1) * capacity]
        sums[0, place : place + 1, :] = jnp.sum(jnp.where(pick, own, 0.0), axis=0, keepdims=True)


def input_kernel(capacity, side, pos, grad_gate_pre, grad_up_pre, weight_gate, weight_up, *refs):
    outs, values = refs[:4], refs[4]
    terms = dot(grad_gate_pre[...], weight_gate[...], LAST)
    values[...] = (terms + dot(grad_up_pre[...], weight_up[...], LAST)).astype(BF16)
    scatter_rows(side[0], pos, values, outs, capacity)


def gather_body(tokens, grad_out, gates, expert_ids, w_gate, w_up, w_down):
    expert_count = lax.axis_size("expert")
    tok_count, top_count = expert_ids.shape
    capacity = tok_count * top_count * 4 // (3 * expert_count)
    width = tokens.shape[1]
    half = width // 2
    column = expert_count // 4
    features = 2 * width
    hidden = w_gate.shape[2]
    step_rows = 4 * capacity
    slots = column * step_rows
    me = lax.axis_index("expert")
    side = lax.axis_index("tensor").astype(jnp.int32).reshape(1)

    core_pairs = [(e, e ^ 1) for e in range(expert_count)]
    chip_pairs = [(e, e ^ 2) for e in range(expert_count)]

    def swap_core(value):
        return lax.ppermute(value, "expert", core_pairs)

    def swap_pair(value):
        return lax.ppermute(value, "expert", chip_pairs)

    def swap_side(value):
        return lax.ppermute(value, "tensor", [(0, 1), (1, 0)])

    def shift(value, step):
        return lax.ppermute(
            value, "expert", [(e, (e + 4 * step) % expert_count) for e in range(expert_count)]
        )

    def spread(rows, start):
        own = after(jnp.stack([rows[:, :half], rows[:, half:]]), *start)
        parts = [own] + [shift(own, step) for step in range(1, column)]
        a = jnp.stack([part[0] for part in parts])
        b = jnp.stack([part[1] for part in parts])
        a = jnp.stack([a, swap_side(a)])
        b = jnp.stack([b, swap_pair(b)])
        far_a = swap_pair(a)
        far_b = swap_side(b)
        pieces = (a, far_a, swap_core(a), swap_core(far_a), b, far_b, swap_core(b), swap_core(far_b))
        return pieces, parts

    def spread_routing():
        own = jnp.concatenate([expert_ids.astype(F32), gates], axis=1).T
        all_parts = jnp.stack([own] + [shift(own, step) for step in range(1, column)])
        all_parts = jnp.stack([all_parts, swap_pair(all_parts)], axis=1)
        all_parts = jnp.concatenate([all_parts, swap_core(all_parts)], axis=1)
        named = all_parts[:, :, :top_count] == me.astype(F32)
        gate = jnp.sum(jnp.where(named, all_parts[:, :, top_count:], 0.0), axis=2)
        member = jnp.any(named, axis=2)
        upto = jnp.triu(jnp.ones((tok_count, tok_count), BF16))
        count = jnp.dot(member.astype(BF16), upto, preferred_element_type=F32)
        return jnp.where(member, count - 1.0, -1.0), gate

    def add(*terms):
        return sum(term.astype(F32) for term in terms)

    def collect(outs):
        own_a, other_a, own_b, other_b = outs
        core_a, core_b = swap_core(other_a), swap_core(other_b)
        first_a = swap_pair(add(own_a[1], core_a[1]).astype(BF16))
        first_b = swap_side(add(own_b[1], core_b[1]).astype(BF16))
        second_a = swap_side(add(own_a[0, 1], core_a[0, 1], first_a[1]).astype(BF16))
        second_b = swap_pair(add(own_b[0, 1], core_b[0, 1], first_b[1]).astype(BF16))
        a = add(own_a[0, 0], core_a[0, 0], first_a[0], second_a)
        b = add(own_b[0, 0], core_b[0, 0], first_b[0], second_b)
        both = jnp.stack([a, b], axis=1)
        total = both[0]
        for step in range(1, column):
            total = total + shift(both[step].astype(BF16), column - step).astype(F32)
        return jnp.concatenate([total[0], total[1]], axis=1).astype(BF16)

    table = pl.BlockSpec((1, 4, tok_count), lambda i, s: (i, 0, 0))
    piece = pl.BlockSpec((2, 1, tok_count, half), lambda i, s: (0, i, 0, 0))
    out_piece = pl.BlockSpec((2, 2, 1, tok_count, half), lambda i, s: (0, 0, i, 0, 0))

    def rows_of(size):
        return pl.BlockSpec((step_rows, size), lambda i, s: (i, 0))

    def whole(*shape):
        return pl.BlockSpec(shape, lambda i, s: (0, 0), pipeline_mode=pl.Buffered(1))

    def kernel(run, macs, in_specs, outs, scratch=()):
        return pl.pallas_call(
            functools.partial(run, capacity),
            out_shape=[shape for shape, _ in outs],
            grid_spec=pltpu.PrefetchScalarGridSpec(
                num_scalar_prefetch=1,
                grid=(column,),
                in_specs=in_specs,
                out_specs=[spec for _, spec in outs],
                scratch_shapes=scratch,
            ),
            compiler_params=pltpu.CompilerParams(vmem_limit_bytes=40 * 1024 * 1024),
            cost_estimate=pl.CostEstimate(
                flops=2 * macs, bytes_accessed=16 * 1024 * 1024, transcendentals=0
            ),
        )

    def shaped(shape, dtype):
        return jax.ShapeDtypeStruct(shape, dtype)

    row_out = (shaped((slots, features), BF16), rows_of(features))
    hidden_f32 = (shaped((slots, hidden), F32), rows_of(hidden))
    hidden_bf = (shaped((slots, hidden), BF16), rows_of(hidden))
    piece_outs = [(shaped((2, 2, column, tok_count, half), BF16), out_piece)] * 4
    macs = slots * features * hidden
    values = [pltpu.VMEM((step_rows, features), BF16)]

    weight_gate, weight_up, weight_down = w_gate[0], w_up[0], w_down[0]
    wide = whole(features, hidden)
    tall = whole(hidden, features)

    token_pieces, token_parts = spread(tokens, ())
    pos, gate = spread_routing()
    grad_pieces, _ = spread(grad_out, token_parts)

    rows, gate_pre, up_pre, scaled = kernel(
        up_kernel,
        2 * macs,
        [table, table] + [piece] * 8 + [wide, wide],
        [row_out, hidden_f32, hidden_f32, hidden_bf],
    )(side, pos, gate, *token_pieces, weight_gate, weight_up)
    mix_out = kernel(
        mix_kernel, macs, [table, rows_of(hidden), tall], piece_outs, values
    )(side, pos, scaled, weight_down)
    mixed = collect(mix_out)
    grad_rows, grad_gate_pre, grad_up_pre, token_sums = kernel(
        back_kernel,
        macs,
        [table, table] + [piece] * 8 + [tall, rows_of(hidden), rows_of(hidden)],
        [row_out, hidden_bf, hidden_bf, (shaped((column, 4, tok_count), F32), table)],
    )(side, pos, gate, *grad_pieces, weight_down, gate_pre, up_pre)
    input_out = kernel(
        input_kernel,
        2 * macs,
        [table, rows_of(hidden), rows_of(hidden), wide, wide],
        piece_outs,
        values,
    )(side, pos, grad_gate_pre, grad_up_pre, weight_gate, weight_up)
    grad_tokens = collect(input_out)

    token_sums = token_sums + swap_side(token_sums)
    block = jnp.arange(expert_count)
    place = (me // 4 - block // 4) % column * 4 + ((me ^ block) % 2) * 2 + ((me ^ block) // 2) % 2
    token_sums = token_sums.reshape(expert_count, tok_count)[place]
    expert_sums = lax.all_to_all(token_sums, "expert", split_axis=0, concat_axis=0, tiled=True)
    chosen = expert_ids[None] == jnp.arange(expert_count, dtype=jnp.int32)[:, None, None]
    grad_gates = jnp.sum(jnp.where(chosen, expert_sums[:, :, None], 0.0), axis=0)

    grad_down = dot(scaled, grad_rows, FIRST).astype(BF16)[None]
    grad_gate = dot(rows, grad_gate_pre, FIRST).astype(BF16)[None]
    grad_up = dot(rows, grad_up_pre, FIRST).astype(BF16)[None]
    return (mixed, grad_tokens, grad_gates, grad_gate, grad_up, grad_down)


def body(tokens, grad_out, gates, expert_ids, w_gate, w_up, w_down):
    expert_count = lax.axis_size("expert")
    tok_count, top_count = expert_ids.shape
    slot_total = tok_count * top_count * 4 // (3 * expert_count) * expert_count
    gathers = expert_count * tok_count <= 2 * slot_total
    shaped = lax.axis_size("tensor") == 2 and expert_count % 4 == 0
    plan = gather_body if gathers and shaped else slots_body
    return plan(tokens, grad_out, gates, expert_ids, w_gate, w_up, w_down)


def solution(mesh):
    placed = (
        P("expert", "tensor"),
        P("expert", "tensor"),
        P("expert", None),
        P("expert", None),
        P("expert", None, "tensor"),
        P("expert", None, "tensor"),
        P("expert", "tensor", None),
    )
    return jax.shard_map(
        body,
        mesh=mesh,
        in_specs=placed,
        out_specs=(
            P("expert", "tensor"),
            P("expert", "tensor"),
            P("expert", None),
            P("expert", None, "tensor"),
            P("expert", None, "tensor"),
            P("expert", "tensor", None),
        ),
        check_vma=False,
    )
```

```python
import functools

import jax
import jax.numpy as jnp
from jax import lax
from jax.experimental import pallas as pl
from jax.experimental.pallas import tpu as pltpu
from jax.sharding import PartitionSpec as P

F32 = jnp.float32
BF16 = jnp.bfloat16
MEBIBYTE = 1024 * 1024


def slots_body(tokens, grad_out, gates, expert_ids, w_gate, w_up, w_down):
    expert_count = lax.axis_size("expert")
    tok_count = expert_ids.shape[0]
    top_count = expert_ids.shape[1]
    capacity = tok_count * top_count * 4 // (3 * expert_count)
    slot_total = expert_count * capacity
    flat_ids = expert_ids.reshape(-1)
    member = (flat_ids[:, None] == jnp.arange(expert_count, dtype=jnp.int32)[None, :]).astype(
        jnp.int32
    )
    earlier = jnp.cumsum(member, axis=0) - member
    position = jnp.sum(earlier * member, axis=1)
    slot_index = flat_ids * capacity + position
    pair_token = jnp.arange(tok_count * top_count, dtype=jnp.int32) // top_count
    pair_gate = gates.reshape(-1)[:, None]

    def pack(rows, scaled):
        picked = rows[pair_token]
        if scaled:
            picked = (pair_gate * picked.astype(jnp.float32)).astype(jnp.bfloat16)
        buffer = jnp.zeros((slot_total, rows.shape[1]), jnp.bfloat16).at[slot_index].set(picked)
        return buffer.reshape(expert_count, capacity, rows.shape[1])

    def dispatch(rows, scaled):
        arrived = lax.all_to_all(
            pack(rows, scaled), "expert", split_axis=0, concat_axis=0, tiled=True
        )
        arrived = arrived.reshape(slot_total, rows.shape[1])
        return lax.all_gather(arrived, "tensor", axis=1, tiled=True)

    def give_back(partial_value):
        shares = lax.psum_scatter(partial_value, "tensor", scatter_dimension=1, tiled=True).astype(
            jnp.bfloat16
        )
        width = shares.shape[1]
        shares = shares.reshape(expert_count, capacity, width)
        returned = lax.all_to_all(shares, "expert", split_axis=0, concat_axis=0, tiled=True)
        return returned.reshape(slot_total, width)[slot_index].reshape(tok_count, top_count, width)

    weight_gate = w_gate[0]
    weight_up = w_up[0]
    weight_down = w_down[0]
    full_rows = dispatch(tokens, False)
    gate_pre = jnp.dot(full_rows, weight_gate, preferred_element_type=jnp.float32)
    up_pre = jnp.dot(full_rows, weight_up, preferred_element_type=jnp.float32)
    sig = jax.nn.sigmoid(gate_pre)
    act = (gate_pre * sig * up_pre).astype(jnp.bfloat16)
    outputs = give_back(jnp.dot(act, weight_down, preferred_element_type=jnp.float32)).astype(
        jnp.float32
    )
    mixed = jnp.sum(gates[:, :, None] * outputs, axis=1).astype(jnp.bfloat16)
    gate_terms = jnp.sum(grad_out.astype(jnp.float32)[:, None, :] * outputs, axis=2)
    grad_gates = lax.psum(gate_terms, "tensor")
    grad_rows = dispatch(grad_out, True)
    contract_last = (((1,), (1,)), ((), ()))
    contract_first = (((0,), (0,)), ((), ()))
    grad_act = lax.dot_general(
        grad_rows, weight_down, contract_last, preferred_element_type=jnp.float32
    )
    grad_gate_pre = (grad_act * up_pre * sig * (1.0 + gate_pre * (1.0 - sig))).astype(jnp.bfloat16)
    grad_up_pre = (grad_act * gate_pre * sig).astype(jnp.bfloat16)
    grad_down = lax.dot_general(
        act, grad_rows, contract_first, preferred_element_type=jnp.float32
    ).astype(jnp.bfloat16)
    grad_gate = lax.dot_general(
        full_rows, grad_gate_pre, contract_first, preferred_element_type=jnp.float32
    ).astype(jnp.bfloat16)
    grad_up = lax.dot_general(
        full_rows, grad_up_pre, contract_first, preferred_element_type=jnp.float32
    ).astype(jnp.bfloat16)
    input_terms = lax.dot_general(
        grad_gate_pre, weight_gate, contract_last, preferred_element_type=jnp.float32
    ) + lax.dot_general(grad_up_pre, weight_up, contract_last, preferred_element_type=jnp.float32)
    input_pairs = give_back(input_terms).astype(jnp.float32)
    grad_tokens = jnp.sum(input_pairs, axis=1).astype(jnp.bfloat16)
    return (mixed, grad_tokens, grad_gates, grad_gate[None], grad_up[None], grad_down[None])


LAST = (((1,), (1,)), ((), ()))
FIRST = (((0,), (0,)), ((), ()))


def dot(left, right, dims=(((1,), (0,)), ((), ()))):
    return lax.dot_general(left, right, dims, preferred_element_type=F32)


def together(*values):
    return lax.optimization_barrier(values)


def picks(pos, place, capacity):
    row = pos[0, place : place + 1, :]
    slot = lax.broadcasted_iota(jnp.int32, (capacity, row.shape[1]), 0).astype(F32)
    return row == slot


def column_of(side, far, start, features, half):
    return pl.multiple_of((side ^ far) * (features // 2) + start, half)


def gather_rows(side, pos, pieces, rows, capacity):
    half = pieces[0].shape[-1]
    features = rows.shape[1]
    for core in range(2):
        for pair in range(2):
            place = 2 * core + pair
            pick = picks(pos, place, capacity).astype(BF16)
            at = pl.ds(place * capacity, capacity)
            for far in range(2):
                for chunk in range(len(pieces) // 8):
                    column = column_of(side, far, 2 * chunk * half, features, half)
                    a = pieces[8 * chunk + 2 * core + pair][far, 0]
                    b = pieces[8 * chunk + 4 + 2 * core + far][pair, 0]
                    rows[at, pl.ds(column, half)] = dot(pick, a).astype(BF16)
                    rows[at, pl.ds(column + half, half)] = dot(pick, b).astype(BF16)


def gate_rows(pos, gate, capacity):
    out = []
    for place in range(4):
        pick = picks(pos, place, capacity)
        out.append(jnp.sum(jnp.where(pick, gate[0, place : place + 1, :], 0.0), axis=1, keepdims=True))
    return jnp.concatenate(out, axis=0)


def scatter_rows(side, pos, values, outs, capacity):
    half = outs[0].shape[-1]
    features = values.shape[1]
    for core in range(2):
        for pair in range(2):
            place = 2 * core + pair
            pick = picks(pos, place, capacity).astype(BF16)
            at = pl.ds(place * capacity, capacity)
            for far in range(2):
                column = column_of(side, far, 0, features, half)
                a = dot(pick, values[at, pl.ds(column, half)], FIRST)
                outs[core][0, pair, far, 0] = a.astype(BF16)
                b = dot(pick, values[at, pl.ds(column + half, half)], FIRST)
                outs[core][1, far, pair, 0] = b.astype(BF16)


def up_kernel(capacity, side, pos, gate, *refs):
    pieces, (weight_gate, weight_up, rows, gate_pre, up_pre, scaled) = refs[:-6], refs[-6:]
    gather_rows(side[0], pos, pieces, rows, capacity)
    gates = gate_rows(pos, gate, capacity)
    got = rows[...]
    pre = dot(got, weight_gate[...], LAST)
    up = dot(got, weight_up[...], LAST)
    gate_pre[...] = pre
    up_pre[...] = up
    scaled[...] = (gates * (pre * jax.nn.sigmoid(pre) * up)).astype(BF16)


def mix_kernel(capacity, side, pos, scaled, weight_down, *refs):
    outs, values = refs[:-1], refs[-1]
    values[...] = dot(scaled[...], weight_down[...]).astype(BF16)
    scatter_rows(side[0], pos, values, outs, capacity)


def back_kernel(capacity, side, pos, gate, *refs):
    pieces, (weight_down, gate_pre, up_pre, rows, grad_gate_pre, grad_up_pre, sums) = refs[:-7], refs[-7:]
    gather_rows(side[0], pos, pieces, rows, capacity)
    gates = gate_rows(pos, gate, capacity)
    plain = dot(rows[...], weight_down[...], LAST)
    pre, up = gate_pre[...], up_pre[...]
    sig = jax.nn.sigmoid(pre)
    silu = pre * sig
    row_sums = jnp.sum(silu * up * plain, axis=1, keepdims=True)
    grad_act = gates * plain
    grad_gate_pre[...] = (grad_act * up * sig * (1.0 + pre * (1.0 - sig))).astype(BF16)
    grad_up_pre[...] = (grad_act * silu).astype(BF16)
    for place in range(4):
        pick = picks(pos, place, capacity)
        own = row_sums[place * capacity : (place + 1) * capacity]
        sums[0, place : place + 1, :] = jnp.sum(jnp.where(pick, own, 0.0), axis=0, keepdims=True)


def input_kernel(capacity, side, pos, grad_gate_pre, grad_up_pre, *refs):
    weights, outs, values = refs[:4], refs[4:-1], refs[-1]
    span = weights[0].shape[1]
    for at in range(2):
        terms = dot(grad_gate_pre[...], weights[at][...])
        terms = terms + dot(grad_up_pre[...], weights[2 + at][...])
        values[:, at * span : (at + 1) * span] = terms.astype(BF16)
    scatter_rows(side[0], pos, values, outs, capacity)


def weight_kernel(pairs, *refs):
    lefts, rows, outs, turned = refs[:pairs], refs[pairs], refs[pairs + 1 : 2 * pairs + 1], refs[2 * pairs + 1 :]

    @pl.when(pl.program_id(0) == 0)
    def _():
        for left, flat in zip(lefts, turned):
            flat[...] = left[...].T

    for flat, out in zip(turned, outs):
        out[...] = dot(flat[...], rows[...]).astype(BF16)


def gather_body(tokens, grad_out, gates, expert_ids, w_gate, w_up, w_down):
    expert_count = lax.axis_size("expert")
    tok_count, top_count = expert_ids.shape
    capacity = tok_count * top_count * 4 // (3 * expert_count)
    width = tokens.shape[1]
    half = width // 2
    column = expert_count // 4
    features = 2 * width
    hidden = w_gate.shape[2]
    step_rows = 4 * capacity
    slots = column * step_rows
    me = lax.axis_index("expert")
    side = lax.axis_index("tensor").astype(jnp.int32).reshape(1)

    core_pairs = [(e, e ^ 1) for e in range(expert_count)]
    chip_pairs = [(e, e ^ 2) for e in range(expert_count)]

    def swap_core(value):
        return lax.ppermute(value, "expert", core_pairs)

    def swap_pair(value):
        return lax.ppermute(value, "expert", chip_pairs)

    def swap_side(value):
        return lax.ppermute(value, "tensor", [(0, 1), (1, 0)])

    def shift(value, step):
        return lax.ppermute(
            value, "expert", [(e, (e + 4 * step) % expert_count) for e in range(expert_count)]
        )

    def routing_rows(width):
        high = lax.reduce_precision(gates, 8, 7)
        middle = lax.reduce_precision(gates - high, 8, 7)
        low = gates - high - middle
        values = jnp.concatenate([expert_ids.astype(F32), high, middle, low], axis=1).T.astype(BF16)
        rows = -(-values.size // (8 * width)) * 8
        return jnp.pad(values.reshape(-1), (0, rows * width - values.size)).reshape(rows, width)

    def column_parts(own):
        return [own] + [shift(own, step) for step in range(1, column)]

    def halves(rows):
        size = rows.shape[1] // 2
        return jnp.stack([rows[:, :size], rows[:, size:]])

    def halves_of(parts):
        return [jnp.stack([part[at] for part in parts]) for at in range(2)]

    def across(a, b):
        return swap_side(a), swap_pair(b)

    def over(a, b):
        return swap_pair(a), swap_side(b)

    def cores(values):
        return tuple(swap_core(value) for value in values)

    def stacks(near, far):
        return tuple(jnp.stack(both) for both in zip(near, far))

    def routing_tables(parts):
        size = 4 * top_count * tok_count
        parts = parts.reshape(4, column, -1)[:, :, :size].reshape(4, column, 4, top_count, tok_count)
        parts = parts.swapaxes(0, 1).astype(F32)
        named = parts[:, :, 0] == me.astype(F32)
        of_all = parts[:, :, 1] + parts[:, :, 2] + parts[:, :, 3]
        gate = jnp.sum(jnp.where(named, of_all, 0.0), axis=2)
        member = jnp.any(named, axis=2)
        upto = jnp.triu(jnp.ones((tok_count, tok_count), BF16))
        count = jnp.dot(member.astype(BF16), upto, preferred_element_type=F32)
        return jnp.where(member, count - 1.0, -1.0), gate

    def sums_of_experts(token_sums):
        block = jnp.arange(expert_count)
        place = (me // 4 - block // 4) % column * 4 + ((me ^ block) % 2) * 2 + ((me ^ block) // 2) % 2
        token_sums = token_sums.reshape(expert_count, tok_count)[place]
        return lax.all_to_all(token_sums, "expert", split_axis=0, concat_axis=0, tiled=True)

    def add(*terms):
        return sum(term.astype(F32) for term in terms)

    def sent_first(own, core):
        return add(own[0, 1], core[0, 1]).astype(BF16), add(own[1, 1], core[1, 1]).astype(BF16)

    def sent_second(own, core, first):
        a = add(own[0, 0, 1], core[0, 0, 1], first[0][1]).astype(BF16)
        return a, add(own[1, 0, 1], core[1, 0, 1], first[1][1]).astype(BF16)

    def sent_column(own, core, first, second):
        a = add(own[0, 0, 0], core[0, 0, 0], first[0][0], second[0])
        b = add(own[1, 0, 0], core[1, 0, 0], first[1][0], second[1])
        return jnp.stack([a, b], axis=1)

    def from_column(both):
        return [shift(both[step].astype(BF16), column - step) for step in range(1, column)]

    def column_sum(own, received):
        total = add(own, *received)
        return jnp.concatenate([total[0], total[1]], axis=1).astype(BF16)

    small = pl.CostEstimate(flops=1 << 20, bytes_accessed=1 << 16, transcendentals=0)
    table = pl.BlockSpec((1, 4, tok_count), lambda i, s: (i, 0, 0))

    def piece_of(piece, chunk=None):
        block = (2, 1, *piece.shape[-2:])
        if chunk is None:
            return pl.BlockSpec(block, lambda i, s: (0, i, 0, 0))
        return pl.BlockSpec((None, *block), lambda i, s: (chunk, 0, i, 0, 0))

    def sums_out(columns):
        block = (2, 2, 2, 1, tok_count, columns)
        spec = pl.BlockSpec(block, lambda i, s: (0, 0, 0, i, 0, 0))
        return [(shaped((2, 2, 2, column, tok_count, columns), BF16), spec)] * 2

    def rows_of(size):
        return pl.BlockSpec((step_rows, size), lambda i, s: (i, 0))

    def whole(*shape):
        return pl.BlockSpec(shape, lambda i, s: (0, 0), pipeline_mode=pl.Buffered(1))

    def kernel(run, in_specs, outs, scratch=(), mebibytes=26):
        return pl.pallas_call(
            functools.partial(run, capacity),
            out_shape=[shape for shape, _ in outs],
            grid_spec=pltpu.PrefetchScalarGridSpec(
                num_scalar_prefetch=1,
                grid=(column,),
                in_specs=in_specs,
                out_specs=[spec for _, spec in outs],
                scratch_shapes=scratch,
            ),
            compiler_params=pltpu.CompilerParams(vmem_limit_bytes=mebibytes * MEBIBYTE),
            cost_estimate=small,
        )

    def weight_grads(rows, *lefts):
        span = features // 4
        held = pl.BlockSpec((slots, hidden), lambda i: (0, 0), pipeline_mode=pl.Buffered(1))
        columns = pl.BlockSpec((slots, span), lambda i: (0, i))
        result = pl.BlockSpec((hidden, span), lambda i: (0, i))
        return pl.pallas_call(
            functools.partial(weight_kernel, len(lefts)),
            out_shape=[shaped((hidden, features), BF16)] * len(lefts),
            grid=(features // span,),
            in_specs=[held] * len(lefts) + [columns],
            out_specs=[result] * len(lefts),
            scratch_shapes=[pltpu.VMEM((hidden, slots), BF16)] * len(lefts),
            compiler_params=pltpu.CompilerParams(vmem_limit_bytes=26 * MEBIBYTE),
            cost_estimate=small,
        )(*lefts, rows)

    def shaped(shape, dtype):
        return jax.ShapeDtypeStruct(shape, dtype)

    row_out = (shaped((slots, features), BF16), rows_of(features))
    hidden_f32 = (shaped((slots, hidden), F32), rows_of(hidden))
    hidden_bf = (shaped((slots, hidden), BF16), rows_of(hidden))
    values = [pltpu.VMEM((step_rows, features), BF16)]

    weight_gate, weight_up, weight_down = w_gate[0].T, w_up[0].T, w_down[0]
    weight = whole(hidden, features)

    token_rows = jnp.concatenate([tokens[:, :half], tokens[:, half:], routing_rows(half)])
    own_1, own_2 = halves(grad_out[:, :half]), halves(grad_out[:, half:])
    with jax.named_scope("column_tokens"):
        token_parts = column_parts(token_rows)
        token_parts, own_1, own_2 = together(token_parts, own_1, own_2)
        near_a = jnp.stack([part[:tok_count] for part in token_parts])
        near_b = jnp.stack([part[tok_count:] for part in token_parts])
    with jax.named_scope("across_tokens"):
        far_a, far_b = across(near_a, near_b)
        parts_1 = column_parts(own_1)
        far_a, far_b, parts_1, own_2 = together(far_a, far_b, parts_1, own_2)
        near_a = jnp.stack([near_a, far_a])
        routing = jnp.stack([near_b[:, tok_count:], far_b[:, tok_count:]])
        near_b = jnp.stack([near_b[:, :tok_count], far_b[:, :tok_count]])
    with jax.named_scope("over_tokens"):
        far_a, far_b = over(near_a, near_b)
        core_a, core_b = cores((near_a, near_b))
        parts_2 = column_parts(own_2)
        far_a, far_b, core_a, core_b, parts_2, core_routing = together(
            far_a, far_b, core_a, core_b, parts_2, swap_core(routing)
        )
        pos, gate = routing_tables(jnp.stack([routing, core_routing]))
    with jax.named_scope("across_grads"):
        far_core_a, far_core_b = cores((far_a, far_b))
        grads_1, grads_2 = halves_of(parts_1), halves_of(parts_2)
        grads_a, grads_b = jnp.stack([grads_1[0], grads_2[0]]), jnp.stack([grads_1[1], grads_2[1]])
        far_grads = across(grads_a, grads_b)
        far_core_a, far_core_b, pos, gate = together(far_core_a, far_core_b, pos, gate)
    pieces = (near_a, far_a, core_a, far_core_a, near_b, far_b, core_b, far_core_b)
    rows, gate_pre, up_pre, scaled = kernel(
        up_kernel,
        [table, table] + [piece_of(piece) for piece in pieces] + [weight, weight],
        [row_out, hidden_f32, hidden_f32, hidden_bf],
        mebibytes=58,
    )(side, pos, gate, *pieces, weight_gate, weight_up)
    far_grads, scaled = together(far_grads, scaled)
    near_a = jnp.stack([grads_a, far_grads[0]], axis=1)
    near_b = jnp.stack([grads_b, far_grads[1]], axis=1)
    with jax.named_scope("over_grads_1"):
        far_1 = over(near_a[0], near_b[0])
        core_a, core_b = cores((near_a, near_b))
    mix_own, mix_other = kernel(mix_kernel, [table, rows_of(hidden), weight], sums_out(half), values)(
        side, pos, scaled, weight_down
    )
    far_1, core_a, core_b, near_a, near_b, mix_other = together(
        far_1, core_a, core_b, near_a, near_b, mix_other
    )
    with jax.named_scope("over_grads_2"):
        far_2 = over(near_a[1], near_b[1])
    with jax.named_scope("cores_mixed"):
        mix_core = swap_core(mix_other)
        mix_send = sent_first(mix_own, mix_core)
        far_core_1 = cores(far_1)
    far_core_1, mix_send = together(far_core_1, mix_send)
    with jax.named_scope("over_mixed"):
        mix_first = over(*mix_send)
    far_2, mix_send = together(far_2, mix_send)
    with jax.named_scope("cores_grads"):
        far_core_2 = cores(far_2)
    pieces = [
        piece
        for chunk, far, far_core in ((0, far_1, far_core_1), (1, far_2, far_core_2))
        for at, near, core in ((0, near_a, core_a), (1, near_b, core_b))
        for piece in ((near, chunk), (far[at], None), (core, chunk), (far_core[at], None))
    ]
    grad_rows, grad_gate_pre, grad_up_pre, token_sums = kernel(
        back_kernel,
        [table, table] + [piece_of(*piece) for piece in pieces] + [weight, rows_of(hidden), rows_of(hidden)],
        [row_out, hidden_bf, hidden_bf, (shaped((column, 4, tok_count), F32), table)],
    )(side, pos, gate, *(piece for piece, _ in pieces), weight_down, gate_pre, up_pre)

    def input_terms(chunk, *hidden_grads):
        columns = [
            pl.BlockSpec((hidden, half), lambda i, s, at=at: (0, 2 * at + chunk), pipeline_mode=pl.Buffered(1))
            for at in range(2)
        ]
        return kernel(
            input_kernel,
            [table, rows_of(hidden), rows_of(hidden)] + columns * 2,
            sums_out(half // 2),
            [pltpu.VMEM((step_rows, width), BF16)],
        )(side, pos, *hidden_grads, weight_gate, weight_gate, weight_up, weight_up)

    own_1, other_1 = input_terms(0, grad_gate_pre, grad_up_pre)
    own_2, other_2 = input_terms(1, grad_gate_pre, grad_up_pre)
    mix_first, other_1, other_2, token_sums = together(mix_first, other_1, other_2, token_sums)
    with jax.named_scope("across_mixed"):
        mix_send = sent_second(mix_own, mix_core, mix_first)
        mix_second = across(*mix_send)
    with jax.named_scope("cores_inputs"):
        core_1, core_2 = cores((other_1, other_2))
    with jax.named_scope("gates"):
        token_sums = token_sums + swap_side(token_sums)
    send_1, send_2 = sent_first(own_1, core_1), sent_first(own_2, core_2)
    scaled, mix_send = together(scaled, mix_send)
    (grad_down,) = weight_grads(grad_rows, scaled)
    mix_second, send_1, send_2, token_sums, grad_down = together(
        mix_second, send_1, send_2, token_sums, grad_down
    )
    with jax.named_scope("over_inputs_1"):
        first_1 = over(*send_1)
    with jax.named_scope("column_mixed"):
        mix_both = sent_column(mix_own, mix_core, mix_first, mix_second)
        mix_received = from_column(mix_both)
    first_1, mix_both = together(first_1, mix_both)
    with jax.named_scope("inputs_1_and_2"):
        send_1 = sent_second(own_1, core_1, first_1)
        to_side = jnp.concatenate([send_1[0][None], send_2[1]])
        to_pair = jnp.concatenate([send_1[1][None], send_2[0]])
        from_side, from_pair = swap_side(to_side), swap_pair(to_pair)
    token_sums, grad_gate_pre, to_side, to_pair = together(token_sums, grad_gate_pre, to_side, to_pair)
    grad_gate, grad_up = weight_grads(rows, grad_gate_pre, grad_up_pre)
    with jax.named_scope("gates"):
        expert_sums = sums_of_experts(token_sums)
    from_side, from_pair, mix_received, grad_gate, grad_up = together(
        from_side, from_pair, mix_received, grad_gate, grad_up
    )
    second_1, first_2 = (from_side[0], from_pair[0]), (from_pair[1:], from_side[1:])
    with jax.named_scope("across_inputs_2"):
        send_2 = sent_second(own_2, core_2, first_2)
        second_2 = across(*send_2)
    second_1, send_2 = together(second_1, send_2)
    with jax.named_scope("column_inputs_1"):
        both_1 = sent_column(own_1, core_1, first_1, second_1)
        received_1 = from_column(both_1)
    mix_received, both_1 = together(mix_received, both_1)
    mixed = column_sum(mix_both[0], mix_received)
    second_2, mixed, expert_sums = together(second_2, mixed, expert_sums)
    with jax.named_scope("column_inputs_2"):
        both_2 = sent_column(own_2, core_2, first_2, second_2)
        received_2 = from_column(both_2)
    both_1, both_2 = together(both_1, both_2)
    grad_tokens_1 = column_sum(both_1[0], received_1)
    grad_tokens = jnp.concatenate([grad_tokens_1, column_sum(both_2[0], received_2)], axis=1)

    chosen = expert_ids[None] == jnp.arange(expert_count, dtype=jnp.int32)[:, None, None]
    grad_gates = jnp.sum(jnp.where(chosen, expert_sums[:, :, None], 0.0), axis=0)

    grad_gate, grad_up, grad_down = grad_gate.T[None], grad_up.T[None], grad_down[None]
    return (mixed, grad_tokens, grad_gates, grad_gate, grad_up, grad_down)


def body(tokens, grad_out, gates, expert_ids, w_gate, w_up, w_down):
    expert_count = lax.axis_size("expert")
    tok_count, top_count = expert_ids.shape
    slot_total = tok_count * top_count * 4 // (3 * expert_count) * expert_count
    gathers = expert_count * tok_count <= 2 * slot_total
    shaped = lax.axis_size("tensor") == 2 and expert_count % 4 == 0 and expert_count <= 256
    plan = gather_body if gathers and shaped else slots_body
    return plan(tokens, grad_out, gates, expert_ids, w_gate, w_up, w_down)


def solution(mesh):
    placed = (
        P("expert", "tensor"),
        P("expert", "tensor"),
        P("expert", None),
        P("expert", None),
        P("expert", None, "tensor"),
        P("expert", None, "tensor"),
        P("expert", "tensor", None),
    )
    return jax.shard_map(
        body,
        mesh=mesh,
        in_specs=placed,
        out_specs=(
            P("expert", "tensor"),
            P("expert", "tensor"),
            P("expert", None),
            P("expert", None, "tensor"),
            P("expert", None, "tensor"),
            P("expert", "tensor", None),
        ),
        check_vma=False,
    )
```

```python
import functools

import jax
import jax.numpy as jnp
from jax import lax
from jax.experimental import pallas as pl
from jax.experimental.pallas import tpu as pltpu
from jax.sharding import PartitionSpec as P

F32 = jnp.float32
BF16 = jnp.bfloat16
MEBIBYTE = 1024 * 1024


def slots_body(tokens, grad_out, gates, expert_ids, w_gate, w_up, w_down):
    expert_count = lax.axis_size("expert")
    tok_count = expert_ids.shape[0]
    top_count = expert_ids.shape[1]
    capacity = tok_count * top_count * 4 // (3 * expert_count)
    slot_total = expert_count * capacity
    flat_ids = expert_ids.reshape(-1)
    member = (flat_ids[:, None] == jnp.arange(expert_count, dtype=jnp.int32)[None, :]).astype(
        jnp.int32
    )
    earlier = jnp.cumsum(member, axis=0) - member
    position = jnp.sum(earlier * member, axis=1)
    slot_index = flat_ids * capacity + position
    pair_token = jnp.arange(tok_count * top_count, dtype=jnp.int32) // top_count
    pair_gate = gates.reshape(-1)[:, None]

    def pack(rows, scaled):
        picked = rows[pair_token]
        if scaled:
            picked = (pair_gate * picked.astype(jnp.float32)).astype(jnp.bfloat16)
        buffer = jnp.zeros((slot_total, rows.shape[1]), jnp.bfloat16).at[slot_index].set(picked)
        return buffer.reshape(expert_count, capacity, rows.shape[1])

    def dispatch(rows, scaled):
        arrived = lax.all_to_all(
            pack(rows, scaled), "expert", split_axis=0, concat_axis=0, tiled=True
        )
        arrived = arrived.reshape(slot_total, rows.shape[1])
        return lax.all_gather(arrived, "tensor", axis=1, tiled=True)

    def give_back(partial_value):
        shares = lax.psum_scatter(partial_value, "tensor", scatter_dimension=1, tiled=True).astype(
            jnp.bfloat16
        )
        width = shares.shape[1]
        shares = shares.reshape(expert_count, capacity, width)
        returned = lax.all_to_all(shares, "expert", split_axis=0, concat_axis=0, tiled=True)
        return returned.reshape(slot_total, width)[slot_index].reshape(tok_count, top_count, width)

    weight_gate = w_gate[0]
    weight_up = w_up[0]
    weight_down = w_down[0]
    full_rows = dispatch(tokens, False)
    gate_pre = jnp.dot(full_rows, weight_gate, preferred_element_type=jnp.float32)
    up_pre = jnp.dot(full_rows, weight_up, preferred_element_type=jnp.float32)
    sig = jax.nn.sigmoid(gate_pre)
    act = (gate_pre * sig * up_pre).astype(jnp.bfloat16)
    outputs = give_back(jnp.dot(act, weight_down, preferred_element_type=jnp.float32)).astype(
        jnp.float32
    )
    mixed = jnp.sum(gates[:, :, None] * outputs, axis=1).astype(jnp.bfloat16)
    gate_terms = jnp.sum(grad_out.astype(jnp.float32)[:, None, :] * outputs, axis=2)
    grad_gates = lax.psum(gate_terms, "tensor")
    grad_rows = dispatch(grad_out, True)
    contract_last = (((1,), (1,)), ((), ()))
    contract_first = (((0,), (0,)), ((), ()))
    grad_act = lax.dot_general(
        grad_rows, weight_down, contract_last, preferred_element_type=jnp.float32
    )
    grad_gate_pre = (grad_act * up_pre * sig * (1.0 + gate_pre * (1.0 - sig))).astype(jnp.bfloat16)
    grad_up_pre = (grad_act * gate_pre * sig).astype(jnp.bfloat16)
    grad_down = lax.dot_general(
        act, grad_rows, contract_first, preferred_element_type=jnp.float32
    ).astype(jnp.bfloat16)
    grad_gate = lax.dot_general(
        full_rows, grad_gate_pre, contract_first, preferred_element_type=jnp.float32
    ).astype(jnp.bfloat16)
    grad_up = lax.dot_general(
        full_rows, grad_up_pre, contract_first, preferred_element_type=jnp.float32
    ).astype(jnp.bfloat16)
    input_terms = lax.dot_general(
        grad_gate_pre, weight_gate, contract_last, preferred_element_type=jnp.float32
    ) + lax.dot_general(grad_up_pre, weight_up, contract_last, preferred_element_type=jnp.float32)
    input_pairs = give_back(input_terms).astype(jnp.float32)
    grad_tokens = jnp.sum(input_pairs, axis=1).astype(jnp.bfloat16)
    return (mixed, grad_tokens, grad_gates, grad_gate[None], grad_up[None], grad_down[None])


LAST = (((1,), (1,)), ((), ()))
FIRST = (((0,), (0,)), ((), ()))


def dot(left, right, dims=(((1,), (0,)), ((), ()))):
    return lax.dot_general(left, right, dims, preferred_element_type=F32)


def together(*values):
    return lax.optimization_barrier(values)


def picks(pos, place, capacity):
    row = pos[0, place : place + 1, :]
    slot = lax.broadcasted_iota(jnp.int32, (capacity, row.shape[1]), 0).astype(F32)
    return row == slot


def column_of(side, far, start, features, half):
    return pl.multiple_of((side ^ far) * (features // 2) + start, half)


def gather_rows(side, pos, pieces, rows, capacity):
    half = pieces[0].shape[-1]
    features = rows.shape[1]
    for core in range(2):
        for pair in range(2):
            place = 2 * core + pair
            pick = picks(pos, place, capacity).astype(BF16)
            at = pl.ds(place * capacity, capacity)
            for far in range(2):
                for chunk in range(len(pieces) // 8):
                    column = column_of(side, far, 2 * chunk * half, features, half)
                    a = pieces[8 * chunk + 2 * core + pair][far, 0]
                    b = pieces[8 * chunk + 4 + 2 * core + far][pair, 0]
                    rows[at, pl.ds(column, half)] = dot(pick, a).astype(BF16)
                    rows[at, pl.ds(column + half, half)] = dot(pick, b).astype(BF16)


def gate_rows(pos, gate, capacity):
    out = []
    for place in range(4):
        pick = picks(pos, place, capacity)
        out.append(jnp.sum(jnp.where(pick, gate[0, place : place + 1, :], 0.0), axis=1, keepdims=True))
    return jnp.concatenate(out, axis=0)


def scatter_rows(side, pos, values, outs, capacity):
    half = outs[0].shape[-1]
    features = values.shape[1]
    for core in range(2):
        for pair in range(2):
            place = 2 * core + pair
            pick = picks(pos, place, capacity).astype(BF16)
            at = pl.ds(place * capacity, capacity)
            for far in range(2):
                column = column_of(side, far, 0, features, half)
                a = dot(pick, values[at, pl.ds(column, half)], FIRST)
                outs[core][0, pair, far, 0] = a.astype(BF16)
                b = dot(pick, values[at, pl.ds(column + half, half)], FIRST)
                outs[core][1, far, pair, 0] = b.astype(BF16)


def up_kernel(capacity, side, pos, gate, *refs):
    pieces, (weight_gate, weight_up, rows, gate_pre, up_pre, scaled) = refs[:-6], refs[-6:]
    gather_rows(side[0], pos, pieces, rows, capacity)
    gates = gate_rows(pos, gate, capacity)
    got = rows[...]
    pre = dot(got, weight_gate[...], LAST)
    up = dot(got, weight_up[...], LAST)
    gate_pre[...] = pre
    up_pre[...] = up
    scaled[...] = (gates * (pre * jax.nn.sigmoid(pre) * up)).astype(BF16)


def mix_kernel(capacity, side, pos, scaled, weight_down, *refs):
    outs, values = refs[:-1], refs[-1]
    values[...] = dot(scaled[...], weight_down[...]).astype(BF16)
    scatter_rows(side[0], pos, values, outs, capacity)


def back_kernel(capacity, side, pos, gate, *refs):
    pieces, (weight_down, gate_pre, up_pre, rows, grad_gate_pre, grad_up_pre, sums) = refs[:-7], refs[-7:]
    gather_rows(side[0], pos, pieces, rows, capacity)
    gates = gate_rows(pos, gate, capacity)
    plain = dot(rows[...], weight_down[...], LAST)
    pre, up = gate_pre[...], up_pre[...]
    sig = jax.nn.sigmoid(pre)
    silu = pre * sig
    row_sums = jnp.sum(silu * up * plain, axis=1, keepdims=True)
    grad_act = gates * plain
    grad_gate_pre[...] = (grad_act * up * sig * (1.0 + pre * (1.0 - sig))).astype(BF16)
    grad_up_pre[...] = (grad_act * silu).astype(BF16)
    for place in range(4):
        pick = picks(pos, place, capacity)
        own = row_sums[place * capacity : (place + 1) * capacity]
        sums[0, place : place + 1, :] = jnp.sum(jnp.where(pick, own, 0.0), axis=0, keepdims=True)


def input_kernel(capacity, side, pos, grad_gate_pre, grad_up_pre, *refs):
    weights, outs, values = refs[:4], refs[4:-1], refs[-1]
    span = weights[0].shape[1]
    for at in range(2):
        terms = dot(grad_gate_pre[...], weights[at][...])
        terms = terms + dot(grad_up_pre[...], weights[2 + at][...])
        values[:, at * span : (at + 1) * span] = terms.astype(BF16)
    scatter_rows(side[0], pos, values, outs, capacity)


def weight_kernel(pairs, *refs):
    lefts, rows, outs, turned = refs[:pairs], refs[pairs], refs[pairs + 1 : 2 * pairs + 1], refs[2 * pairs + 1 :]

    @pl.when(pl.program_id(0) == 0)
    def _():
        for left, flat in zip(lefts, turned):
            flat[...] = left[...].T

    for flat, out in zip(turned, outs):
        out[...] = dot(flat[...], rows[...]).astype(BF16)


def gather_body(tokens, grad_out, gates, expert_ids, w_gate, w_up, w_down):
    expert_count = lax.axis_size("expert")
    tok_count, top_count = expert_ids.shape
    capacity = tok_count * top_count * 4 // (3 * expert_count)
    width = tokens.shape[1]
    half = width // 2
    column = expert_count // 4
    features = 2 * width
    hidden = w_gate.shape[2]
    step_rows = 4 * capacity
    slots = column * step_rows
    me = lax.axis_index("expert")
    side = lax.axis_index("tensor").astype(jnp.int32).reshape(1)

    core_pairs = [(e, e ^ 1) for e in range(expert_count)]
    chip_pairs = [(e, e ^ 2) for e in range(expert_count)]

    def swap_core(value):
        return lax.ppermute(value, "expert", core_pairs)

    def swap_pair(value):
        return lax.ppermute(value, "expert", chip_pairs)

    def swap_side(value):
        return lax.ppermute(value, "tensor", [(0, 1), (1, 0)])

    def shift(value, step):
        return lax.ppermute(
            value, "expert", [(e, (e + 4 * step) % expert_count) for e in range(expert_count)]
        )

    def routing_rows(width):
        high = lax.reduce_precision(gates, 8, 7)
        middle = lax.reduce_precision(gates - high, 8, 7)
        low = gates - high - middle
        values = jnp.concatenate([expert_ids.astype(F32), high, middle, low], axis=1).T.astype(BF16)
        rows = -(-values.size // (8 * width)) * 8
        return jnp.pad(values.reshape(-1), (0, rows * width - values.size)).reshape(rows, width)

    def column_parts(own):
        return [own] + [shift(own, step) for step in range(1, column)]

    def relayed_parts(own):
        if column != 4:
            return column_parts(own)
        one, three = shift(own, 1), shift(own, 3)
        inner = [(e, (e + 8) % expert_count) for e in range(expert_count) if e // 4 in (0, 3)]
        two = lax.ppermute(own, "expert", inner)
        outer = [(e, e - 4) for e in range(4, 8)] + [(e, e + 4) for e in range(8, 12)]
        passed = lax.ppermute(jnp.where(me // 4 == 1, three, one), "expert", outer)
        return [own, one, jnp.where((me // 4 == 1) | (me // 4 == 2), two, passed), three]

    def halves(rows):
        size = rows.shape[1] // 2
        return jnp.stack([rows[:, :size], rows[:, size:]])

    def halves_of(parts):
        return [jnp.stack([part[at] for part in parts]) for at in range(2)]

    def across(a, b):
        return swap_side(a), swap_pair(b)

    def over(a, b):
        return swap_pair(a), swap_side(b)

    def cores(values):
        return tuple(swap_core(value) for value in values)

    def stacks(near, far):
        return tuple(jnp.stack(both) for both in zip(near, far))

    def routing_tables(parts):
        size = 4 * top_count * tok_count
        parts = parts.reshape(4, column, -1)[:, :, :size].reshape(4, column, 4, top_count, tok_count)
        parts = parts.swapaxes(0, 1).astype(F32)
        named = parts[:, :, 0] == me.astype(F32)
        of_all = parts[:, :, 1] + parts[:, :, 2] + parts[:, :, 3]
        gate = jnp.sum(jnp.where(named, of_all, 0.0), axis=2)
        member = jnp.any(named, axis=2)
        upto = jnp.triu(jnp.ones((tok_count, tok_count), BF16))
        count = jnp.dot(member.astype(BF16), upto, preferred_element_type=F32)
        return jnp.where(member, count - 1.0, -1.0), gate

    def sums_of_experts(token_sums):
        block = jnp.arange(expert_count)
        place = (me // 4 - block // 4) % column * 4 + ((me ^ block) % 2) * 2 + ((me ^ block) // 2) % 2
        token_sums = token_sums.reshape(expert_count, tok_count)[place]
        return lax.all_to_all(token_sums, "expert", split_axis=0, concat_axis=0, tiled=True)

    def add(*terms):
        return sum(term.astype(F32) for term in terms)

    def sent_first(own, core):
        return add(own[0, 1], core[0, 1]).astype(BF16), add(own[1, 1], core[1, 1]).astype(BF16)

    def sent_second(own, core, first):
        a = add(own[0, 0, 1], core[0, 0, 1], first[0][1]).astype(BF16)
        return a, add(own[1, 0, 1], core[1, 0, 1], first[1][1]).astype(BF16)

    def sent_column(own, core, first, second):
        a = add(own[0, 0, 0], core[0, 0, 0], first[0][0], second[0])
        b = add(own[1, 0, 0], core[1, 0, 0], first[1][0], second[1])
        return jnp.stack([a, b], axis=1)

    def from_column(both):
        return [shift(both[step].astype(BF16), column - step) for step in range(1, column)]

    def column_sum(own, received):
        total = add(own, *received)
        return jnp.concatenate([total[0], total[1]], axis=1).astype(BF16)

    small = pl.CostEstimate(flops=1 << 20, bytes_accessed=1 << 16, transcendentals=0)
    table = pl.BlockSpec((1, 4, tok_count), lambda i, s: (i, 0, 0))

    def piece_of(piece, chunk=None):
        block = (2, 1, *piece.shape[-2:])
        if chunk is None:
            return pl.BlockSpec(block, lambda i, s: (0, i, 0, 0))
        return pl.BlockSpec((None, *block), lambda i, s: (chunk, 0, i, 0, 0))

    def sums_out(columns):
        block = (2, 2, 2, 1, tok_count, columns)
        spec = pl.BlockSpec(block, lambda i, s: (0, 0, 0, i, 0, 0))
        return [(shaped((2, 2, 2, column, tok_count, columns), BF16), spec)] * 2

    def rows_of(size):
        return pl.BlockSpec((step_rows, size), lambda i, s: (i, 0))

    def whole(*shape):
        return pl.BlockSpec(shape, lambda i, s: (0, 0), pipeline_mode=pl.Buffered(1))

    def kernel(run, in_specs, outs, scratch=(), mebibytes=26):
        return pl.pallas_call(
            functools.partial(run, capacity),
            out_shape=[shape for shape, _ in outs],
            grid_spec=pltpu.PrefetchScalarGridSpec(
                num_scalar_prefetch=1,
                grid=(column,),
                in_specs=in_specs,
                out_specs=[spec for _, spec in outs],
                scratch_shapes=scratch,
            ),
            compiler_params=pltpu.CompilerParams(vmem_limit_bytes=mebibytes * MEBIBYTE),
            cost_estimate=small,
        )

    def weight_grads(rows, *lefts):
        span = features // 4
        held = pl.BlockSpec((slots, hidden), lambda i: (0, 0), pipeline_mode=pl.Buffered(1))
        columns = pl.BlockSpec((slots, span), lambda i: (0, i))
        result = pl.BlockSpec((hidden, span), lambda i: (0, i))
        return pl.pallas_call(
            functools.partial(weight_kernel, len(lefts)),
            out_shape=[shaped((hidden, features), BF16)] * len(lefts),
            grid=(features // span,),
            in_specs=[held] * len(lefts) + [columns],
            out_specs=[result] * len(lefts),
            scratch_shapes=[pltpu.VMEM((hidden, slots), BF16)] * len(lefts),
            compiler_params=pltpu.CompilerParams(vmem_limit_bytes=26 * MEBIBYTE),
            cost_estimate=small,
        )(*lefts, rows)

    def shaped(shape, dtype):
        return jax.ShapeDtypeStruct(shape, dtype)

    row_out = (shaped((slots, features), BF16), rows_of(features))
    hidden_f32 = (shaped((slots, hidden), F32), rows_of(hidden))
    hidden_bf = (shaped((slots, hidden), BF16), rows_of(hidden))
    values = [pltpu.VMEM((step_rows, features), BF16)]

    weight_gate, weight_up, weight_down = w_gate[0].T, w_up[0].T, w_down[0]
    weight = whole(hidden, features)

    token_rows = jnp.concatenate([tokens[:, :half], tokens[:, half:], routing_rows(half)])
    own_1, own_2 = halves(grad_out[:, :half]), halves(grad_out[:, half:])
    with jax.named_scope("column_tokens"):
        token_parts = relayed_parts(token_rows)
        token_parts, own_1, own_2 = together(token_parts, own_1, own_2)
        near_a = jnp.stack([part[:tok_count] for part in token_parts])
        near_b = jnp.stack([part[tok_count:] for part in token_parts])
    with jax.named_scope("across_tokens"):
        far_a, far_b = across(near_a, near_b)
        parts_1 = column_parts(own_1)
        far_a, far_b, parts_1, own_2 = together(far_a, far_b, parts_1, own_2)
        near_a = jnp.stack([near_a, far_a])
        routing = jnp.stack([near_b[:, tok_count:], far_b[:, tok_count:]])
        near_b = jnp.stack([near_b[:, :tok_count], far_b[:, :tok_count]])
    with jax.named_scope("over_tokens"):
        far_a, far_b = over(near_a, near_b)
        core_a, core_b = cores((near_a, near_b))
        parts_2 = column_parts(own_2)
        pos, gate = routing_tables(jnp.stack([routing, swap_core(routing)]))
        far_a, far_b, core_a, core_b, parts_2, pos, gate = together(
            far_a, far_b, core_a, core_b, parts_2, pos, gate
        )
    with jax.named_scope("across_grads"):
        far_core_a, far_core_b = cores((far_a, far_b))
        grads_1, grads_2 = halves_of(parts_1), halves_of(parts_2)
        grads_a, grads_b = jnp.stack([grads_1[0], grads_2[0]]), jnp.stack([grads_1[1], grads_2[1]])
        far_grads = across(grads_a, grads_b)
        far_core_a, far_core_b, pos = together(far_core_a, far_core_b, pos)
    pieces = (near_a, far_a, core_a, far_core_a, near_b, far_b, core_b, far_core_b)
    rows, gate_pre, up_pre, scaled = kernel(
        up_kernel,
        [table, table] + [piece_of(piece) for piece in pieces] + [weight, weight],
        [row_out, hidden_f32, hidden_f32, hidden_bf],
        mebibytes=58,
    )(side, pos, gate, *pieces, weight_gate, weight_up)
    far_grads, scaled = together(far_grads, scaled)
    near_a = jnp.stack([grads_a, far_grads[0]], axis=1)
    near_b = jnp.stack([grads_b, far_grads[1]], axis=1)
    with jax.named_scope("over_grads_1"):
        far_1 = over(near_a[0], near_b[0])
        core_a, core_b = cores((near_a, near_b))
    mix_own, mix_other = kernel(mix_kernel, [table, rows_of(hidden), weight], sums_out(half), values)(
        side, pos, scaled, weight_down
    )
    far_1, core_a, core_b, near_a, near_b, mix_other = together(
        far_1, core_a, core_b, near_a, near_b, mix_other
    )
    with jax.named_scope("over_grads_2"):
        far_2 = over(near_a[1], near_b[1])
    with jax.named_scope("cores_mixed"):
        mix_core = swap_core(mix_other)
        mix_send = sent_first(mix_own, mix_core)
        far_core_1 = cores(far_1)
    far_core_1, mix_send = together(far_core_1, mix_send)
    with jax.named_scope("over_mixed"):
        mix_first = over(*mix_send)
    far_2, mix_send = together(far_2, mix_send)
    with jax.named_scope("cores_grads"):
        far_core_2 = cores(far_2)
    pieces = [
        piece
        for chunk, far, far_core in ((0, far_1, far_core_1), (1, far_2, far_core_2))
        for at, near, core in ((0, near_a, core_a), (1, near_b, core_b))
        for piece in ((near, chunk), (far[at], None), (core, chunk), (far_core[at], None))
    ]
    grad_rows, grad_gate_pre, grad_up_pre, token_sums = kernel(
        back_kernel,
        [table, table] + [piece_of(*piece) for piece in pieces] + [weight, rows_of(hidden), rows_of(hidden)],
        [row_out, hidden_bf, hidden_bf, (shaped((column, 4, tok_count), F32), table)],
    )(side, pos, gate, *(piece for piece, _ in pieces), weight_down, gate_pre, up_pre)

    def input_terms(chunk, *hidden_grads):
        columns = [
            pl.BlockSpec((hidden, half), lambda i, s, at=at: (0, 2 * at + chunk), pipeline_mode=pl.Buffered(1))
            for at in range(2)
        ]
        return kernel(
            input_kernel,
            [table, rows_of(hidden), rows_of(hidden)] + columns * 2,
            sums_out(half // 2),
            [pltpu.VMEM((step_rows, width), BF16)],
        )(side, pos, *hidden_grads, weight_gate, weight_gate, weight_up, weight_up)

    own_1, other_1 = input_terms(0, grad_gate_pre, grad_up_pre)
    own_2, other_2 = input_terms(1, grad_gate_pre, grad_up_pre)
    with jax.named_scope("gates"):
        token_sums = token_sums + swap_side(token_sums)
    mix_first, other_1, other_2, token_sums = together(mix_first, other_1, other_2, token_sums)
    with jax.named_scope("across_mixed"):
        mix_send = sent_second(mix_own, mix_core, mix_first)
        mix_second = across(*mix_send)
    with jax.named_scope("cores_inputs"):
        core_1, core_2 = cores((other_1, other_2))
    send_1, send_2 = sent_first(own_1, core_1), sent_first(own_2, core_2)
    scaled, mix_send = together(scaled, mix_send)
    (grad_down,) = weight_grads(grad_rows, scaled)
    send_1, send_2, grad_down = together(send_1, send_2, grad_down)
    with jax.named_scope("over_inputs_1"):
        first_1 = over(*send_1)
    with jax.named_scope("column_mixed"):
        mix_both = sent_column(mix_own, mix_core, mix_first, mix_second)
        mix_received = from_column(mix_both)
    first_1, send_2, mix_received[::2] = together(first_1, send_2, mix_received[::2])
    with jax.named_scope("across_inputs_1"):
        send_1 = sent_second(own_1, core_1, first_1)
        second_1 = across(*send_1)
    with jax.named_scope("over_inputs_2"):
        send_1, send_2 = together(send_1, send_2)
        first_2 = over(*send_2)
    grad_gate_pre, send_2 = together(grad_gate_pre, send_2)
    grad_gate, grad_up = weight_grads(rows, grad_gate_pre, grad_up_pre)
    second_1, mix_received, grad_gate, grad_up = together(second_1, mix_received, grad_gate, grad_up)
    with jax.named_scope("column_inputs_1"):
        both_1 = sent_column(own_1, core_1, first_1, second_1)
        received_1 = from_column(both_1)
    first_2, both_1 = together(first_2, both_1)
    with jax.named_scope("across_inputs_2"):
        send_2 = sent_second(own_2, core_2, first_2)
        second_2 = across(*send_2)
    mix_received, send_2 = together(mix_received, send_2)
    mixed = column_sum(mix_both[0], mix_received)
    second_2, mixed = together(second_2, mixed)
    with jax.named_scope("column_inputs_2"):
        both_2 = sent_column(own_2, core_2, first_2, second_2)
        received_2 = from_column(both_2)
    token_sums, both_1, both_2 = together(token_sums, both_1, both_2)
    with jax.named_scope("gates"):
        expert_sums = sums_of_experts(token_sums)
    grad_tokens_1 = column_sum(both_1[0], received_1)
    received_2, expert_sums, grad_tokens_1 = together(received_2, expert_sums, grad_tokens_1)
    grad_tokens = jnp.concatenate([grad_tokens_1, column_sum(both_2[0], received_2)], axis=1)

    chosen = expert_ids[None] == jnp.arange(expert_count, dtype=jnp.int32)[:, None, None]
    grad_gates = jnp.sum(jnp.where(chosen, expert_sums[:, :, None], 0.0), axis=0)

    grad_gate, grad_up, grad_down = grad_gate.T[None], grad_up.T[None], grad_down[None]
    return (mixed, grad_tokens, grad_gates, grad_gate, grad_up, grad_down)


def body(tokens, grad_out, gates, expert_ids, w_gate, w_up, w_down):
    expert_count = lax.axis_size("expert")
    tok_count, top_count = expert_ids.shape
    slot_total = tok_count * top_count * 4 // (3 * expert_count) * expert_count
    gathers = expert_count * tok_count <= 2 * slot_total
    shaped = lax.axis_size("tensor") == 2 and expert_count % 4 == 0 and expert_count <= 256
    plan = gather_body if gathers and shaped else slots_body
    return plan(tokens, grad_out, gates, expert_ids, w_gate, w_up, w_down)


def solution(mesh):
    placed = (
        P("expert", "tensor"),
        P("expert", "tensor"),
        P("expert", None),
        P("expert", None),
        P("expert", None, "tensor"),
        P("expert", None, "tensor"),
        P("expert", "tensor", None),
    )
    return jax.shard_map(
        body,
        mesh=mesh,
        in_specs=placed,
        out_specs=(
            P("expert", "tensor"),
            P("expert", "tensor"),
            P("expert", None),
            P("expert", None, "tensor"),
            P("expert", None, "tensor"),
            P("expert", "tensor", None),
        ),
        check_vma=False,
    )
```

```python
import functools

import jax
import jax.numpy as jnp
from jax import lax
from jax.experimental import pallas as pl
from jax.experimental.pallas import tpu as pltpu
from jax.sharding import PartitionSpec as P

F32 = jnp.float32
BF16 = jnp.bfloat16
MEBIBYTE = 1024 * 1024


def slots_body(tokens, grad_out, gates, expert_ids, w_gate, w_up, w_down):
    expert_count = lax.axis_size("expert")
    tok_count = expert_ids.shape[0]
    top_count = expert_ids.shape[1]
    capacity = tok_count * top_count * 4 // (3 * expert_count)
    slot_total = expert_count * capacity
    flat_ids = expert_ids.reshape(-1)
    member = (flat_ids[:, None] == jnp.arange(expert_count, dtype=jnp.int32)[None, :]).astype(
        jnp.int32
    )
    earlier = jnp.cumsum(member, axis=0) - member
    position = jnp.sum(earlier * member, axis=1)
    slot_index = flat_ids * capacity + position
    pair_token = jnp.arange(tok_count * top_count, dtype=jnp.int32) // top_count
    pair_gate = gates.reshape(-1)[:, None]

    def pack(rows, scaled):
        picked = rows[pair_token]
        if scaled:
            picked = (pair_gate * picked.astype(jnp.float32)).astype(jnp.bfloat16)
        buffer = jnp.zeros((slot_total, rows.shape[1]), jnp.bfloat16).at[slot_index].set(picked)
        return buffer.reshape(expert_count, capacity, rows.shape[1])

    def dispatch(rows, scaled):
        arrived = lax.all_to_all(
            pack(rows, scaled), "expert", split_axis=0, concat_axis=0, tiled=True
        )
        arrived = arrived.reshape(slot_total, rows.shape[1])
        return lax.all_gather(arrived, "tensor", axis=1, tiled=True)

    def give_back(partial_value):
        shares = lax.psum_scatter(partial_value, "tensor", scatter_dimension=1, tiled=True).astype(
            jnp.bfloat16
        )
        width = shares.shape[1]
        shares = shares.reshape(expert_count, capacity, width)
        returned = lax.all_to_all(shares, "expert", split_axis=0, concat_axis=0, tiled=True)
        return returned.reshape(slot_total, width)[slot_index].reshape(tok_count, top_count, width)

    weight_gate = w_gate[0]
    weight_up = w_up[0]
    weight_down = w_down[0]
    full_rows = dispatch(tokens, False)
    gate_pre = jnp.dot(full_rows, weight_gate, preferred_element_type=jnp.float32)
    up_pre = jnp.dot(full_rows, weight_up, preferred_element_type=jnp.float32)
    sig = jax.nn.sigmoid(gate_pre)
    act = (gate_pre * sig * up_pre).astype(jnp.bfloat16)
    outputs = give_back(jnp.dot(act, weight_down, preferred_element_type=jnp.float32)).astype(
        jnp.float32
    )
    mixed = jnp.sum(gates[:, :, None] * outputs, axis=1).astype(jnp.bfloat16)
    gate_terms = jnp.sum(grad_out.astype(jnp.float32)[:, None, :] * outputs, axis=2)
    grad_gates = lax.psum(gate_terms, "tensor")
    grad_rows = dispatch(grad_out, True)
    contract_last = (((1,), (1,)), ((), ()))
    contract_first = (((0,), (0,)), ((), ()))
    grad_act = lax.dot_general(
        grad_rows, weight_down, contract_last, preferred_element_type=jnp.float32
    )
    grad_gate_pre = (grad_act * up_pre * sig * (1.0 + gate_pre * (1.0 - sig))).astype(jnp.bfloat16)
    grad_up_pre = (grad_act * gate_pre * sig).astype(jnp.bfloat16)
    grad_down = lax.dot_general(
        act, grad_rows, contract_first, preferred_element_type=jnp.float32
    ).astype(jnp.bfloat16)
    grad_gate = lax.dot_general(
        full_rows, grad_gate_pre, contract_first, preferred_element_type=jnp.float32
    ).astype(jnp.bfloat16)
    grad_up = lax.dot_general(
        full_rows, grad_up_pre, contract_first, preferred_element_type=jnp.float32
    ).astype(jnp.bfloat16)
    input_terms = lax.dot_general(
        grad_gate_pre, weight_gate, contract_last, preferred_element_type=jnp.float32
    ) + lax.dot_general(grad_up_pre, weight_up, contract_last, preferred_element_type=jnp.float32)
    input_pairs = give_back(input_terms).astype(jnp.float32)
    grad_tokens = jnp.sum(input_pairs, axis=1).astype(jnp.bfloat16)
    return (mixed, grad_tokens, grad_gates, grad_gate[None], grad_up[None], grad_down[None])


LAST = (((1,), (1,)), ((), ()))
FIRST = (((0,), (0,)), ((), ()))


def dot(left, right, dims=(((1,), (0,)), ((), ()))):
    return lax.dot_general(left, right, dims, preferred_element_type=F32)


def together(*values):
    return lax.optimization_barrier(values)


def picks(pos, place, capacity):
    row = pos[0, place : place + 1, :]
    slot = lax.broadcasted_iota(jnp.int32, (capacity, row.shape[1]), 0).astype(F32)
    return row == slot


def column_of(side, far, start, features, half):
    return pl.multiple_of((side ^ far) * (features // 2) + start, half)


def gather_rows(side, pos, pieces, rows, capacity):
    half = pieces[0].shape[-1]
    features = rows.shape[1]
    for core in range(2):
        for pair in range(2):
            place = 2 * core + pair
            pick = picks(pos, place, capacity).astype(BF16)
            at = pl.ds(place * capacity, capacity)
            for far in range(2):
                for chunk in range(len(pieces) // 8):
                    column = column_of(side, far, 2 * chunk * half, features, half)
                    a = pieces[8 * chunk + 2 * core + pair][far, 0]
                    b = pieces[8 * chunk + 4 + 2 * core + far][pair, 0]
                    rows[at, pl.ds(column, half)] = dot(pick, a).astype(BF16)
                    rows[at, pl.ds(column + half, half)] = dot(pick, b).astype(BF16)


def gate_rows(pos, gate, capacity):
    out = []
    for place in range(4):
        pick = picks(pos, place, capacity)
        out.append(jnp.sum(jnp.where(pick, gate[0, place : place + 1, :], 0.0), axis=1, keepdims=True))
    return jnp.concatenate(out, axis=0)


def scatter_rows(side, pos, values, outs, capacity):
    half = outs[0].shape[-1]
    features = values.shape[1]
    for core in range(2):
        for pair in range(2):
            place = 2 * core + pair
            pick = picks(pos, place, capacity).astype(BF16)
            at = pl.ds(place * capacity, capacity)
            for far in range(2):
                column = column_of(side, far, 0, features, half)
                a = dot(pick, values[at, pl.ds(column, half)], FIRST)
                outs[core][0, pair, far, 0] = a.astype(BF16)
                b = dot(pick, values[at, pl.ds(column + half, half)], FIRST)
                outs[core][1, far, pair, 0] = b.astype(BF16)


def up_kernel(capacity, side, pos, gate, *refs):
    pieces, (weight_gate, weight_up, rows, gate_pre, up_pre, scaled) = refs[:-6], refs[-6:]
    gather_rows(side[0], pos, pieces, rows, capacity)
    gates = gate_rows(pos, gate, capacity)
    got = rows[...]
    pre = dot(got, weight_gate[...], LAST)
    up = dot(got, weight_up[...], LAST)
    gate_pre[...] = pre
    up_pre[...] = up
    scaled[...] = (gates * (pre * jax.nn.sigmoid(pre) * up)).astype(BF16)


def mix_kernel(capacity, side, pos, scaled, weight_down, *refs):
    outs, values = refs[:-1], refs[-1]
    values[...] = dot(scaled[...], weight_down[...]).astype(BF16)
    scatter_rows(side[0], pos, values, outs, capacity)


def back_kernel(capacity, side, pos, gate, *refs):
    pieces, (weight_down, gate_pre, up_pre, rows, grad_gate_pre, grad_up_pre, sums) = refs[:-7], refs[-7:]
    gather_rows(side[0], pos, pieces, rows, capacity)
    gates = gate_rows(pos, gate, capacity)
    plain = dot(rows[...], weight_down[...], LAST)
    pre, up = gate_pre[...], up_pre[...]
    sig = jax.nn.sigmoid(pre)
    silu = pre * sig
    row_sums = jnp.sum(silu * up * plain, axis=1, keepdims=True)
    grad_act = gates * plain
    grad_gate_pre[...] = (grad_act * up * sig * (1.0 + pre * (1.0 - sig))).astype(BF16)
    grad_up_pre[...] = (grad_act * silu).astype(BF16)
    for place in range(4):
        pick = picks(pos, place, capacity)
        own = row_sums[place * capacity : (place + 1) * capacity]
        sums[0, place : place + 1, :] = jnp.sum(jnp.where(pick, own, 0.0), axis=0, keepdims=True)


def input_kernel(capacity, side, pos, grad_gate_pre, grad_up_pre, *refs):
    blocks, outs, values = refs[:-3], refs[-3:-1], refs[-1]
    count = len(blocks) // 2
    span = blocks[0].shape[1]
    for at in range(count):
        terms = dot(grad_gate_pre[...], blocks[at][...])
        terms = terms + dot(grad_up_pre[...], blocks[count + at][...])
        values[:, at * span : (at + 1) * span] = terms.astype(BF16)
    scatter_rows(side[0], pos, values, outs, capacity)


def weight_kernel(pairs, *refs):
    lefts, rows, outs, turned = refs[:pairs], refs[pairs], refs[pairs + 1 : 2 * pairs + 1], refs[2 * pairs + 1 :]

    @pl.when(pl.program_id(0) == 0)
    def _():
        for left, flat in zip(lefts, turned):
            flat[...] = left[...].T

    for flat, out in zip(turned, outs):
        out[...] = dot(flat[...], rows[...]).astype(BF16)


def gather_body(tokens, grad_out, gates, expert_ids, w_gate, w_up, w_down):
    expert_count = lax.axis_size("expert")
    tok_count, top_count = expert_ids.shape
    capacity = tok_count * top_count * 4 // (3 * expert_count)
    width = tokens.shape[1]
    half = width // 2
    column = expert_count // 4
    features = 2 * width
    hidden = w_gate.shape[2]
    step_rows = 4 * capacity
    slots = column * step_rows
    me = lax.axis_index("expert")
    side = lax.axis_index("tensor").astype(jnp.int32).reshape(1)

    core_pairs = [(e, e ^ 1) for e in range(expert_count)]
    chip_pairs = [(e, e ^ 2) for e in range(expert_count)]

    def swap_core(value):
        return lax.ppermute(value, "expert", core_pairs)

    def swap_pair(value):
        return lax.ppermute(value, "expert", chip_pairs)

    def swap_side(value):
        return lax.ppermute(value, "tensor", [(0, 1), (1, 0)])

    def shift(value, step):
        return lax.ppermute(
            value, "expert", [(e, (e + 4 * step) % expert_count) for e in range(expert_count)]
        )

    def routing_rows(width):
        high = lax.reduce_precision(gates, 8, 7)
        middle = lax.reduce_precision(gates - high, 8, 7)
        low = gates - high - middle
        values = jnp.concatenate([expert_ids.astype(F32), high, middle, low], axis=1).T.astype(BF16)
        rows = -(-values.size // (8 * width)) * 8
        return jnp.pad(values.reshape(-1), (0, rows * width - values.size)).reshape(rows, width)

    def column_parts(own):
        return [own] + [shift(own, step) for step in range(1, column)]

    def relayed_parts(own):
        if column != 4:
            return column_parts(own)
        one, three = shift(own, 1), shift(own, 3)
        inner = [(e, (e + 8) % expert_count) for e in range(expert_count) if e // 4 in (0, 3)]
        two = lax.ppermute(own, "expert", inner)
        outer = [(e, e - 4) for e in range(4, 8)] + [(e, e + 4) for e in range(8, 12)]
        passed = lax.ppermute(jnp.where(me // 4 == 1, three, one), "expert", outer)
        return [own, one, jnp.where((me // 4 == 1) | (me // 4 == 2), two, passed), three]

    def halves(rows):
        size = rows.shape[1] // 2
        return jnp.stack([rows[:, :size], rows[:, size:]])

    def halves_of(parts):
        return [jnp.stack([part[at] for part in parts]) for at in range(2)]

    def across(a, b):
        return swap_side(a), swap_pair(b)

    def over(a, b):
        return swap_pair(a), swap_side(b)

    def cores(values):
        return tuple(swap_core(value) for value in values)

    def stacks(near, far):
        return tuple(jnp.stack(both) for both in zip(near, far))

    def routing_tables(parts):
        size = 4 * top_count * tok_count
        parts = parts.reshape(4, column, -1)[:, :, :size].reshape(4, column, 4, top_count, tok_count)
        parts = parts.swapaxes(0, 1).astype(F32)
        named = parts[:, :, 0] == me.astype(F32)
        of_all = parts[:, :, 1] + parts[:, :, 2] + parts[:, :, 3]
        gate = jnp.sum(jnp.where(named, of_all, 0.0), axis=2)
        member = jnp.any(named, axis=2)
        upto = jnp.triu(jnp.ones((tok_count, tok_count), BF16))
        count = jnp.dot(member.astype(BF16), upto, preferred_element_type=F32)
        return jnp.where(member, count - 1.0, -1.0), gate

    def sums_of_experts(token_sums):
        block = jnp.arange(expert_count)
        place = (me // 4 - block // 4) % column * 4 + ((me ^ block) % 2) * 2 + ((me ^ block) // 2) % 2
        token_sums = token_sums.reshape(expert_count, tok_count)[place]
        return lax.all_to_all(token_sums, "expert", split_axis=0, concat_axis=0, tiled=True)

    def add(*terms):
        return sum(term.astype(F32) for term in terms)

    def sent_first(own, core):
        return add(own[0, 1], core[0, 1]).astype(BF16), add(own[1, 1], core[1, 1]).astype(BF16)

    def sent_second(own, core, first):
        a = add(own[0, 0, 1], core[0, 0, 1], first[0][1]).astype(BF16)
        return a, add(own[1, 0, 1], core[1, 0, 1], first[1][1]).astype(BF16)

    def sent_column(own, core, first, second):
        a = add(own[0, 0, 0], core[0, 0, 0], first[0][0], second[0])
        b = add(own[1, 0, 0], core[1, 0, 0], first[1][0], second[1])
        return jnp.stack([a, b], axis=1)

    def from_column(both):
        return [shift(both[step].astype(BF16), column - step) for step in range(1, column)]

    def column_sum(own, received):
        total = add(own, *received)
        return jnp.concatenate([total[0], total[1]], axis=1).astype(BF16)

    small = pl.CostEstimate(flops=1 << 20, bytes_accessed=1 << 16, transcendentals=0)
    table = pl.BlockSpec((1, 4, tok_count), lambda i, s: (i, 0, 0))

    def piece_of(piece, chunk=None):
        block = (2, 1, *piece.shape[-2:])
        if chunk is None:
            return pl.BlockSpec(block, lambda i, s: (0, i, 0, 0))
        return pl.BlockSpec((None, *block), lambda i, s: (chunk, 0, i, 0, 0))

    def sums_out(columns):
        block = (2, 2, 2, 1, tok_count, columns)
        spec = pl.BlockSpec(block, lambda i, s: (0, 0, 0, i, 0, 0))
        return [(shaped((2, 2, 2, column, tok_count, columns), BF16), spec)] * 2

    def rows_of(size):
        return pl.BlockSpec((step_rows, size), lambda i, s: (i, 0))

    def whole(*shape):
        return pl.BlockSpec(shape, lambda i, s: (0, 0), pipeline_mode=pl.Buffered(1))

    def kernel(run, in_specs, outs, scratch=(), mebibytes=22):
        return pl.pallas_call(
            functools.partial(run, capacity),
            out_shape=[shape for shape, _ in outs],
            grid_spec=pltpu.PrefetchScalarGridSpec(
                num_scalar_prefetch=1,
                grid=(column,),
                in_specs=in_specs,
                out_specs=[spec for _, spec in outs],
                scratch_shapes=scratch,
            ),
            compiler_params=pltpu.CompilerParams(vmem_limit_bytes=mebibytes * MEBIBYTE),
            cost_estimate=small,
        )

    def weight_grads(rows, *lefts):
        span = features // 4
        held = pl.BlockSpec((slots, hidden), lambda i: (0, 0), pipeline_mode=pl.Buffered(1))
        columns = pl.BlockSpec((slots, span), lambda i: (0, i))
        result = pl.BlockSpec((hidden, span), lambda i: (0, i))
        return pl.pallas_call(
            functools.partial(weight_kernel, len(lefts)),
            out_shape=[shaped((hidden, features), BF16)] * len(lefts),
            grid=(features // span,),
            in_specs=[held] * len(lefts) + [columns],
            out_specs=[result] * len(lefts),
            scratch_shapes=[pltpu.VMEM((hidden, slots), BF16)] * len(lefts),
            compiler_params=pltpu.CompilerParams(vmem_limit_bytes=14 * MEBIBYTE),
            cost_estimate=small,
        )(*lefts, rows)

    def shaped(shape, dtype):
        return jax.ShapeDtypeStruct(shape, dtype)

    row_out = (shaped((slots, features), BF16), rows_of(features))
    hidden_f32 = (shaped((slots, hidden), F32), rows_of(hidden))
    hidden_bf = (shaped((slots, hidden), BF16), rows_of(hidden))
    values = [pltpu.VMEM((step_rows, features), BF16)]

    weight_gate, weight_up, weight_down = w_gate[0].T, w_up[0].T, w_down[0]
    weight = whole(hidden, features)

    token_rows = jnp.concatenate([tokens[:, :half], tokens[:, half:], routing_rows(half)])
    own_1, own_2 = halves(grad_out[:, :half]), halves(grad_out[:, half:])
    with jax.named_scope("column_tokens"):
        token_parts = relayed_parts(token_rows)
        token_parts, own_1, own_2 = together(token_parts, own_1, own_2)
        near_a = jnp.stack([part[:tok_count] for part in token_parts])
        near_b = jnp.stack([part[tok_count:] for part in token_parts])
    with jax.named_scope("across_tokens"):
        far_a, far_b = across(near_a, near_b)
        parts_1 = column_parts(own_1)
        far_a, far_b, parts_1, own_2 = together(far_a, far_b, parts_1, own_2)
        near_a = jnp.stack([near_a, far_a])
        routing = jnp.stack([near_b[:, tok_count:], far_b[:, tok_count:]])
        near_b = jnp.stack([near_b[:, :tok_count], far_b[:, :tok_count]])
    with jax.named_scope("over_tokens"):
        far_a, far_b = over(near_a, near_b)
        core_a, core_b = cores((near_a, near_b))
        parts_2 = column_parts(own_2)
        pos, gate = routing_tables(jnp.stack([routing, swap_core(routing)]))
        far_a, far_b, core_a, core_b, parts_2, pos, gate = together(
            far_a, far_b, core_a, core_b, parts_2, pos, gate
        )
    with jax.named_scope("across_grads"):
        far_core_a, far_core_b = cores((far_a, far_b))
        grads_1, grads_2 = halves_of(parts_1), halves_of(parts_2)
        grads_a, grads_b = jnp.stack([grads_1[0], grads_2[0]]), jnp.stack([grads_1[1], grads_2[1]])
        far_grads = across(grads_a, grads_b)
        far_core_a, far_core_b, pos = together(far_core_a, far_core_b, pos)
    pieces = (near_a, far_a, core_a, far_core_a, near_b, far_b, core_b, far_core_b)
    rows, gate_pre, up_pre, scaled = kernel(
        up_kernel,
        [table, table] + [piece_of(piece) for piece in pieces] + [weight, weight],
        [row_out, hidden_f32, hidden_f32, hidden_bf],
        mebibytes=58,
    )(side, pos, gate, *pieces, weight_gate, weight_up)
    far_grads, scaled = together(far_grads, scaled)
    near_a = jnp.stack([grads_a, far_grads[0]], axis=1)
    near_b = jnp.stack([grads_b, far_grads[1]], axis=1)
    with jax.named_scope("over_grads_1"):
        far_1 = over(near_a[0], near_b[0])
        core_a, core_b = cores((near_a, near_b))
    mix_own, mix_other = kernel(mix_kernel, [table, rows_of(hidden), weight], sums_out(half), values)(
        side, pos, scaled, weight_down
    )
    far_1, core_a, core_b, near_a, near_b, mix_other = together(
        far_1, core_a, core_b, near_a, near_b, mix_other
    )
    with jax.named_scope("over_grads_2"):
        far_2 = over(near_a[1], near_b[1])
    with jax.named_scope("cores_mixed"):
        mix_core = swap_core(mix_other)
        mix_send = sent_first(mix_own, mix_core)
        far_core_1 = cores(far_1)
    far_core_1, mix_send = together(far_core_1, mix_send)
    with jax.named_scope("over_mixed"):
        mix_first = over(*mix_send)
    far_2, mix_send = together(far_2, mix_send)
    with jax.named_scope("cores_grads"):
        far_core_2 = cores(far_2)
    pieces = [
        piece
        for chunk, far, far_core in ((0, far_1, far_core_1), (1, far_2, far_core_2))
        for at, near, core in ((0, near_a, core_a), (1, near_b, core_b))
        for piece in ((near, chunk), (far[at], None), (core, chunk), (far_core[at], None))
    ]
    grad_rows, grad_gate_pre, grad_up_pre, token_sums = kernel(
        back_kernel,
        [table, table] + [piece_of(*piece) for piece in pieces] + [weight, rows_of(hidden), rows_of(hidden)],
        [row_out, hidden_bf, hidden_bf, (shaped((column, 4, tok_count), F32), table)],
    )(side, pos, gate, *(piece for piece, _ in pieces), weight_down, gate_pre, up_pre)

    def input_terms(quarters):
        span = width // 4
        blocks = [
            pl.BlockSpec((hidden, span), lambda i, s, at=4 * far + quarter: (0, at), pipeline_mode=pl.Buffered(1))
            for far in range(2)
            for quarter in quarters
        ]
        count = len(blocks)
        return kernel(
            input_kernel,
            [table, rows_of(hidden), rows_of(hidden)] + blocks * 2,
            sums_out(len(quarters) * span // 2),
            [pltpu.VMEM((step_rows, count * span), BF16)],
        )(side, pos, grad_gate_pre, grad_up_pre, *[weight_gate] * count, *[weight_up] * count)

    own_1, other_1 = input_terms((0, 1, 2))
    own_2, other_2 = input_terms((3,))
    with jax.named_scope("gates"):
        token_sums = token_sums + swap_side(token_sums)
    mix_first, other_1, other_2, token_sums = together(mix_first, other_1, other_2, token_sums)
    with jax.named_scope("across_mixed"):
        mix_send = sent_second(mix_own, mix_core, mix_first)
        mix_second = across(*mix_send)
    with jax.named_scope("cores_inputs"):
        core_1, core_2 = cores((other_1, other_2))
    send_1, send_2 = sent_first(own_1, core_1), sent_first(own_2, core_2)
    scaled, mix_send = together(scaled, mix_send)
    (grad_down,) = weight_grads(grad_rows, scaled)
    send_1, send_2, grad_down = together(send_1, send_2, grad_down)
    with jax.named_scope("over_inputs_1"):
        first_1 = over(*send_1)
    with jax.named_scope("column_mixed"):
        mix_both = sent_column(mix_own, mix_core, mix_first, mix_second)
        mix_received = from_column(mix_both)
    grad_gate_pre, mix_both = together(grad_gate_pre, mix_both)
    grad_gate, grad_up = weight_grads(rows, grad_gate_pre, grad_up_pre)
    first_1, send_2, mix_received[::2], grad_gate, grad_up = together(
        first_1, send_2, mix_received[::2], grad_gate, grad_up
    )
    with jax.named_scope("across_inputs_1"):
        send_1 = sent_second(own_1, core_1, first_1)
        second_1 = across(*send_1)
    with jax.named_scope("over_inputs_2"):
        send_1, send_2 = together(send_1, send_2)
        first_2 = over(*send_2)
    second_1, mix_received = together(second_1, mix_received)
    with jax.named_scope("column_inputs_1"):
        both_1 = sent_column(own_1, core_1, first_1, second_1)
        received_1 = from_column(both_1)
    first_2, both_1 = together(first_2, both_1)
    with jax.named_scope("across_inputs_2"):
        send_2 = sent_second(own_2, core_2, first_2)
        second_2 = across(*send_2)
    mix_received, send_2 = together(mix_received, send_2)
    mixed = column_sum(mix_both[0], mix_received)
    second_2, mixed = together(second_2, mixed)
    with jax.named_scope("column_inputs_2"):
        both_2 = sent_column(own_2, core_2, first_2, second_2)
        received_2 = from_column(both_2)
    token_sums, both_1, both_2 = together(token_sums, both_1, both_2)
    with jax.named_scope("gates"):
        expert_sums = sums_of_experts(token_sums)
    grad_tokens_1 = column_sum(both_1[0], received_1)
    received_2, expert_sums, grad_tokens_1 = together(received_2, expert_sums, grad_tokens_1)
    grad_tokens = jnp.concatenate([grad_tokens_1, column_sum(both_2[0], received_2)], axis=1)

    chosen = expert_ids[None] == jnp.arange(expert_count, dtype=jnp.int32)[:, None, None]
    grad_gates = jnp.sum(jnp.where(chosen, expert_sums[:, :, None], 0.0), axis=0)

    grad_gate, grad_up, grad_down = grad_gate.T[None], grad_up.T[None], grad_down[None]
    return (mixed, grad_tokens, grad_gates, grad_gate, grad_up, grad_down)


def body(tokens, grad_out, gates, expert_ids, w_gate, w_up, w_down):
    expert_count = lax.axis_size("expert")
    tok_count, top_count = expert_ids.shape
    slot_total = tok_count * top_count * 4 // (3 * expert_count) * expert_count
    gathers = expert_count * tok_count <= 2 * slot_total
    shaped = lax.axis_size("tensor") == 2 and expert_count % 4 == 0 and expert_count <= 256
    plan = gather_body if gathers and shaped else slots_body
    return plan(tokens, grad_out, gates, expert_ids, w_gate, w_up, w_down)


def solution(mesh):
    placed = (
        P("expert", "tensor"),
        P("expert", "tensor"),
        P("expert", None),
        P("expert", None),
        P("expert", None, "tensor"),
        P("expert", None, "tensor"),
        P("expert", "tensor", None),
    )
    return jax.shard_map(
        body,
        mesh=mesh,
        in_specs=placed,
        out_specs=(
            P("expert", "tensor"),
            P("expert", "tensor"),
            P("expert", None),
            P("expert", None, "tensor"),
            P("expert", None, "tensor"),
            P("expert", "tensor", None),
        ),
        check_vma=False,
    )
```

```python
import functools

import jax
import jax.numpy as jnp
from jax import lax
from jax.experimental import pallas as pl
from jax.experimental.pallas import tpu as pltpu
from jax.sharding import PartitionSpec as P

F32 = jnp.float32
BF16 = jnp.bfloat16
MEBIBYTE = 1024 * 1024


def slots_body(tokens, grad_out, gates, expert_ids, w_gate, w_up, w_down):
    expert_count = lax.axis_size("expert")
    tok_count = expert_ids.shape[0]
    top_count = expert_ids.shape[1]
    capacity = tok_count * top_count * 4 // (3 * expert_count)
    slot_total = expert_count * capacity
    flat_ids = expert_ids.reshape(-1)
    member = (flat_ids[:, None] == jnp.arange(expert_count, dtype=jnp.int32)[None, :]).astype(
        jnp.int32
    )
    earlier = jnp.cumsum(member, axis=0) - member
    position = jnp.sum(earlier * member, axis=1)
    slot_index = flat_ids * capacity + position
    pair_token = jnp.arange(tok_count * top_count, dtype=jnp.int32) // top_count
    pair_gate = gates.reshape(-1)[:, None]

    def pack(rows, scaled):
        picked = rows[pair_token]
        if scaled:
            picked = (pair_gate * picked.astype(jnp.float32)).astype(jnp.bfloat16)
        buffer = jnp.zeros((slot_total, rows.shape[1]), jnp.bfloat16).at[slot_index].set(picked)
        return buffer.reshape(expert_count, capacity, rows.shape[1])

    def dispatch(rows, scaled):
        arrived = lax.all_to_all(
            pack(rows, scaled), "expert", split_axis=0, concat_axis=0, tiled=True
        )
        arrived = arrived.reshape(slot_total, rows.shape[1])
        return lax.all_gather(arrived, "tensor", axis=1, tiled=True)

    def give_back(partial_value):
        shares = lax.psum_scatter(partial_value, "tensor", scatter_dimension=1, tiled=True).astype(
            jnp.bfloat16
        )
        width = shares.shape[1]
        shares = shares.reshape(expert_count, capacity, width)
        returned = lax.all_to_all(shares, "expert", split_axis=0, concat_axis=0, tiled=True)
        return returned.reshape(slot_total, width)[slot_index].reshape(tok_count, top_count, width)

    weight_gate = w_gate[0]
    weight_up = w_up[0]
    weight_down = w_down[0]
    full_rows = dispatch(tokens, False)
    gate_pre = jnp.dot(full_rows, weight_gate, preferred_element_type=jnp.float32)
    up_pre = jnp.dot(full_rows, weight_up, preferred_element_type=jnp.float32)
    sig = jax.nn.sigmoid(gate_pre)
    act = (gate_pre * sig * up_pre).astype(jnp.bfloat16)
    outputs = give_back(jnp.dot(act, weight_down, preferred_element_type=jnp.float32)).astype(
        jnp.float32
    )
    mixed = jnp.sum(gates[:, :, None] * outputs, axis=1).astype(jnp.bfloat16)
    gate_terms = jnp.sum(grad_out.astype(jnp.float32)[:, None, :] * outputs, axis=2)
    grad_gates = lax.psum(gate_terms, "tensor")
    grad_rows = dispatch(grad_out, True)
    contract_last = (((1,), (1,)), ((), ()))
    contract_first = (((0,), (0,)), ((), ()))
    grad_act = lax.dot_general(
        grad_rows, weight_down, contract_last, preferred_element_type=jnp.float32
    )
    grad_gate_pre = (grad_act * up_pre * sig * (1.0 + gate_pre * (1.0 - sig))).astype(jnp.bfloat16)
    grad_up_pre = (grad_act * gate_pre * sig).astype(jnp.bfloat16)
    grad_down = lax.dot_general(
        act, grad_rows, contract_first, preferred_element_type=jnp.float32
    ).astype(jnp.bfloat16)
    grad_gate = lax.dot_general(
        full_rows, grad_gate_pre, contract_first, preferred_element_type=jnp.float32
    ).astype(jnp.bfloat16)
    grad_up = lax.dot_general(
        full_rows, grad_up_pre, contract_first, preferred_element_type=jnp.float32
    ).astype(jnp.bfloat16)
    input_terms = lax.dot_general(
        grad_gate_pre, weight_gate, contract_last, preferred_element_type=jnp.float32
    ) + lax.dot_general(grad_up_pre, weight_up, contract_last, preferred_element_type=jnp.float32)
    input_pairs = give_back(input_terms).astype(jnp.float32)
    grad_tokens = jnp.sum(input_pairs, axis=1).astype(jnp.bfloat16)
    return (mixed, grad_tokens, grad_gates, grad_gate[None], grad_up[None], grad_down[None])


LAST = (((1,), (1,)), ((), ()))
FIRST = (((0,), (0,)), ((), ()))


def dot(left, right, dims=(((1,), (0,)), ((), ()))):
    return lax.dot_general(left, right, dims, preferred_element_type=F32)


def together(*values):
    return lax.optimization_barrier(values)


def picks(pos, place, capacity):
    row = pos[0, place : place + 1, :]
    slot = lax.broadcasted_iota(jnp.int32, (capacity, row.shape[1]), 0).astype(F32)
    return row == slot


def column_of(side, far, start, features, half):
    return pl.multiple_of((side ^ far) * (features // 2) + start, half)


def gather_rows(side, pos, pieces, rows, capacity):
    half = pieces[0].shape[-1]
    features = rows.shape[1]
    for core in range(2):
        for pair in range(2):
            place = 2 * core + pair
            pick = picks(pos, place, capacity).astype(BF16)
            at = pl.ds(place * capacity, capacity)
            for far in range(2):
                for chunk in range(len(pieces) // 8):
                    column = column_of(side, far, 2 * chunk * half, features, half)
                    a = pieces[8 * chunk + 2 * core + pair][far, 0]
                    b = pieces[8 * chunk + 4 + 2 * core + far][pair, 0]
                    rows[at, pl.ds(column, half)] = dot(pick, a).astype(BF16)
                    rows[at, pl.ds(column + half, half)] = dot(pick, b).astype(BF16)


def gate_rows(pos, gate, capacity):
    out = []
    for place in range(4):
        pick = picks(pos, place, capacity)
        out.append(jnp.sum(jnp.where(pick, gate[0, place : place + 1, :], 0.0), axis=1, keepdims=True))
    return jnp.concatenate(out, axis=0)


def scatter_rows(side, pos, values, outs, capacity):
    half = outs[0].shape[-1]
    features = values.shape[1]
    for core in range(2):
        for pair in range(2):
            place = 2 * core + pair
            pick = picks(pos, place, capacity).astype(BF16)
            at = pl.ds(place * capacity, capacity)
            for far in range(2):
                column = column_of(side, far, 0, features, half)
                a = dot(pick, values[at, pl.ds(column, half)], FIRST)
                outs[core][0, pair, far, 0] = a.astype(BF16)
                b = dot(pick, values[at, pl.ds(column + half, half)], FIRST)
                outs[core][1, far, pair, 0] = b.astype(BF16)


def up_kernel(capacity, side, pos, gate, *refs):
    pieces, (weight_gate, weight_up, rows, gate_pre, up_pre, scaled) = refs[:-6], refs[-6:]
    gather_rows(side[0], pos, pieces, rows, capacity)
    gates = gate_rows(pos, gate, capacity)
    got = rows[...]
    pre = dot(got, weight_gate[...], LAST)
    up = dot(got, weight_up[...], LAST)
    gate_pre[...] = pre
    up_pre[...] = up
    scaled[...] = (gates * (pre * jax.nn.sigmoid(pre) * up)).astype(BF16)


def mix_kernel(capacity, side, pos, scaled, weight_down, *refs):
    outs, values = refs[:-1], refs[-1]
    values[...] = dot(scaled[...], weight_down[...]).astype(BF16)
    scatter_rows(side[0], pos, values, outs, capacity)


def back_kernel(capacity, side, pos, gate, *refs):
    pieces, (weight_down, gate_pre, up_pre, rows, grad_gate_pre, grad_up_pre, sums) = refs[:-7], refs[-7:]
    gather_rows(side[0], pos, pieces, rows, capacity)
    gates = gate_rows(pos, gate, capacity)
    plain = dot(rows[...], weight_down[...], LAST)
    pre, up = gate_pre[...], up_pre[...]
    sig = jax.nn.sigmoid(pre)
    silu = pre * sig
    row_sums = jnp.sum(silu * up * plain, axis=1, keepdims=True)
    grad_act = gates * plain
    grad_gate_pre[...] = (grad_act * up * sig * (1.0 + pre * (1.0 - sig))).astype(BF16)
    grad_up_pre[...] = (grad_act * silu).astype(BF16)
    for place in range(4):
        pick = picks(pos, place, capacity)
        own = row_sums[place * capacity : (place + 1) * capacity]
        sums[0, place : place + 1, :] = jnp.sum(jnp.where(pick, own, 0.0), axis=0, keepdims=True)


def input_kernel(capacity, side, pos, grad_gate_pre, grad_up_pre, *refs):
    blocks, outs, values = refs[:-3], refs[-3:-1], refs[-1]
    count = len(blocks) // 2
    span = blocks[0].shape[1]
    for at in range(count):
        terms = dot(grad_gate_pre[...], blocks[at][...])
        terms = terms + dot(grad_up_pre[...], blocks[count + at][...])
        values[:, at * span : (at + 1) * span] = terms.astype(BF16)
    scatter_rows(side[0], pos, values, outs, capacity)


def weight_kernel(pairs, *refs):
    lefts, rows, outs, turned = refs[:pairs], refs[pairs], refs[pairs + 1 : 2 * pairs + 1], refs[2 * pairs + 1 :]

    @pl.when(pl.program_id(0) == 0)
    def _():
        for left, flat in zip(lefts, turned):
            flat[...] = left[...].T

    for flat, out in zip(turned, outs):
        out[...] = dot(flat[...], rows[...]).astype(BF16)


def gather_body(tokens, grad_out, gates, expert_ids, w_gate, w_up, w_down):
    expert_count = lax.axis_size("expert")
    tok_count, top_count = expert_ids.shape
    capacity = tok_count * top_count * 4 // (3 * expert_count)
    width = tokens.shape[1]
    half = width // 2
    column = expert_count // 4
    features = 2 * width
    hidden = w_gate.shape[2]
    step_rows = 4 * capacity
    slots = column * step_rows
    me = lax.axis_index("expert")
    side = lax.axis_index("tensor").astype(jnp.int32).reshape(1)

    core_pairs = [(e, e ^ 1) for e in range(expert_count)]
    chip_pairs = [(e, e ^ 2) for e in range(expert_count)]

    def swap_core(value):
        return lax.ppermute(value, "expert", core_pairs)

    def swap_pair(value):
        return lax.ppermute(value, "expert", chip_pairs)

    def swap_side(value):
        return lax.ppermute(value, "tensor", [(0, 1), (1, 0)])

    def shift(value, step):
        return lax.ppermute(
            value, "expert", [(e, (e + 4 * step) % expert_count) for e in range(expert_count)]
        )

    def routing_rows(width):
        high = lax.reduce_precision(gates, 8, 7)
        middle = lax.reduce_precision(gates - high, 8, 7)
        low = gates - high - middle
        values = jnp.concatenate([expert_ids.astype(F32), high, middle, low], axis=1).T.astype(BF16)
        rows = -(-values.size // (8 * width)) * 8
        return jnp.pad(values.reshape(-1), (0, rows * width - values.size)).reshape(rows, width)

    def column_parts(own):
        return [own] + [shift(own, step) for step in range(1, column)]

    def relayed_parts(own):
        if column != 4:
            return column_parts(own)
        one, three = shift(own, 1), shift(own, 3)
        inner = [(e, (e + 8) % expert_count) for e in range(expert_count) if e // 4 in (0, 3)]
        two = lax.ppermute(own, "expert", inner)
        outer = [(e, e - 4) for e in range(4, 8)] + [(e, e + 4) for e in range(8, 12)]
        passed = lax.ppermute(jnp.where(me // 4 == 1, three, one), "expert", outer)
        return [own, one, jnp.where((me // 4 == 1) | (me // 4 == 2), two, passed), three]

    def halves(rows):
        size = rows.shape[1] // 2
        return jnp.stack([rows[:, :size], rows[:, size:]])

    def halves_of(parts):
        return [jnp.stack([part[at] for part in parts]) for at in range(2)]

    def across(a, b):
        return swap_side(a), swap_pair(b)

    def over(a, b):
        return swap_pair(a), swap_side(b)

    def cores(values):
        return tuple(swap_core(value) for value in values)

    def stacks(near, far):
        return tuple(jnp.stack(both) for both in zip(near, far))

    def routing_tables(parts):
        size = 4 * top_count * tok_count
        parts = parts.reshape(4, column, -1)[:, :, :size].reshape(4, column, 4, top_count, tok_count)
        parts = parts.swapaxes(0, 1).astype(F32)
        named = parts[:, :, 0] == me.astype(F32)
        of_all = parts[:, :, 1] + parts[:, :, 2] + parts[:, :, 3]
        gate = jnp.sum(jnp.where(named, of_all, 0.0), axis=2)
        member = jnp.any(named, axis=2)
        upto = jnp.triu(jnp.ones((tok_count, tok_count), BF16))
        count = jnp.dot(member.astype(BF16), upto, preferred_element_type=F32)
        return jnp.where(member, count - 1.0, -1.0), gate

    def sums_of_experts(token_sums):
        block = jnp.arange(expert_count)
        place = (me // 4 - block // 4) % column * 4 + ((me ^ block) % 2) * 2 + ((me ^ block) // 2) % 2
        token_sums = token_sums.reshape(expert_count, tok_count)[place]
        return lax.all_to_all(token_sums, "expert", split_axis=0, concat_axis=0, tiled=True)

    def add(*terms):
        return sum(term.astype(F32) for term in terms)

    def sent_first(own, core):
        return add(own[0, 1], core[0, 1]).astype(BF16), add(own[1, 1], core[1, 1]).astype(BF16)

    def sent_second(own, core, first):
        a = add(own[0, 0, 1], core[0, 0, 1], first[0][1]).astype(BF16)
        return a, add(own[1, 0, 1], core[1, 0, 1], first[1][1]).astype(BF16)

    def sent_column(own, core, first, second):
        a = add(own[0, 0, 0], core[0, 0, 0], first[0][0], second[0])
        b = add(own[1, 0, 0], core[1, 0, 0], first[1][0], second[1])
        return jnp.stack([a, b], axis=1)

    def from_column(both):
        return [shift(both[step].astype(BF16), column - step) for step in range(1, column)]

    def column_sum(own, received):
        total = add(own, *received)
        return jnp.concatenate([total[0], total[1]], axis=1).astype(BF16)

    small = pl.CostEstimate(flops=1 << 20, bytes_accessed=1 << 16, transcendentals=0)
    table = pl.BlockSpec((1, 4, tok_count), lambda i, s: (i, 0, 0))

    def piece_of(piece, chunk=None):
        block = (2, 1, *piece.shape[-2:])
        if chunk is None:
            return pl.BlockSpec(block, lambda i, s: (0, i, 0, 0))
        return pl.BlockSpec((None, *block), lambda i, s: (chunk, 0, i, 0, 0))

    def sums_out(columns):
        block = (2, 2, 2, 1, tok_count, columns)
        spec = pl.BlockSpec(block, lambda i, s: (0, 0, 0, i, 0, 0))
        return [(shaped((2, 2, 2, column, tok_count, columns), BF16), spec)] * 2

    def rows_of(size):
        return pl.BlockSpec((step_rows, size), lambda i, s: (i, 0))

    def whole(*shape):
        return pl.BlockSpec(shape, lambda i, s: (0, 0), pipeline_mode=pl.Buffered(1))

    def kernel(run, in_specs, outs, scratch=(), mebibytes=22):
        return pl.pallas_call(
            functools.partial(run, capacity),
            out_shape=[shape for shape, _ in outs],
            grid_spec=pltpu.PrefetchScalarGridSpec(
                num_scalar_prefetch=1,
                grid=(column,),
                in_specs=in_specs,
                out_specs=[spec for _, spec in outs],
                scratch_shapes=scratch,
            ),
            compiler_params=pltpu.CompilerParams(vmem_limit_bytes=mebibytes * MEBIBYTE),
            cost_estimate=small,
        )

    def weight_grads(rows, *lefts):
        span = features // 4
        held = pl.BlockSpec((slots, hidden), lambda i: (0, 0), pipeline_mode=pl.Buffered(1))
        columns = pl.BlockSpec((slots, span), lambda i: (0, i))
        result = pl.BlockSpec((hidden, span), lambda i: (0, i))
        return pl.pallas_call(
            functools.partial(weight_kernel, len(lefts)),
            out_shape=[shaped((hidden, features), BF16)] * len(lefts),
            grid=(features // span,),
            in_specs=[held] * len(lefts) + [columns],
            out_specs=[result] * len(lefts),
            scratch_shapes=[pltpu.VMEM((hidden, slots), BF16)] * len(lefts),
            compiler_params=pltpu.CompilerParams(vmem_limit_bytes=14 * MEBIBYTE),
            cost_estimate=small,
        )(*lefts, rows)

    def shaped(shape, dtype):
        return jax.ShapeDtypeStruct(shape, dtype)

    row_out = (shaped((slots, features), BF16), rows_of(features))
    hidden_f32 = (shaped((slots, hidden), F32), rows_of(hidden))
    hidden_bf = (shaped((slots, hidden), BF16), rows_of(hidden))
    values = [pltpu.VMEM((step_rows, features), BF16)]

    weight_gate, weight_up, weight_down = w_gate[0].T, w_up[0].T, w_down[0]
    weight = whole(hidden, features)

    token_rows = jnp.concatenate([tokens[:, :half], tokens[:, half:], routing_rows(half)])
    own_1, own_2 = halves(grad_out[:, :half]), halves(grad_out[:, half:])
    with jax.named_scope("column_tokens"):
        token_parts = relayed_parts(token_rows)
        token_parts, own_1, own_2 = together(token_parts, own_1, own_2)
        near_a = jnp.stack([part[:tok_count] for part in token_parts])
        near_b = jnp.stack([part[tok_count:] for part in token_parts])
    with jax.named_scope("across_tokens"):
        far_a, far_b = across(near_a, near_b)
        parts_1 = column_parts(own_1)
        far_a, far_b, parts_1, own_2 = together(far_a, far_b, parts_1, own_2)
        near_a = jnp.stack([near_a, far_a])
        routing = jnp.stack([near_b[:, tok_count:], far_b[:, tok_count:]])
        near_b = jnp.stack([near_b[:, :tok_count], far_b[:, :tok_count]])
    with jax.named_scope("over_tokens"):
        far_a, far_b = over(near_a, near_b)
        core_a, core_b = cores((near_a, near_b))
        parts_2 = column_parts(own_2)
        pos, gate = routing_tables(jnp.stack([routing, swap_core(routing)]))
        far_a, far_b, core_a, core_b, parts_2, pos, gate = together(
            far_a, far_b, core_a, core_b, parts_2, pos, gate
        )
    with jax.named_scope("across_grads"):
        far_core_a, far_core_b = cores((far_a, far_b))
        grads_1, grads_2 = halves_of(parts_1), halves_of(parts_2)
        grads_a, grads_b = jnp.stack([grads_1[0], grads_2[0]]), jnp.stack([grads_1[1], grads_2[1]])
        far_grads = across(grads_a, grads_b)
        far_core_a, far_core_b, pos = together(far_core_a, far_core_b, pos)
    pieces = (near_a, far_a, core_a, far_core_a, near_b, far_b, core_b, far_core_b)
    rows, gate_pre, up_pre, scaled = kernel(
        up_kernel,
        [table, table] + [piece_of(piece) for piece in pieces] + [weight, weight],
        [row_out, hidden_f32, hidden_f32, hidden_bf],
        mebibytes=58,
    )(side, pos, gate, *pieces, weight_gate, weight_up)
    far_grads, scaled = together(far_grads, scaled)
    near_a = jnp.stack([grads_a, far_grads[0]], axis=1)
    near_b = jnp.stack([grads_b, far_grads[1]], axis=1)
    with jax.named_scope("over_grads_1"):
        far_1 = over(near_a[0], near_b[0])
        core_a, core_b = cores((near_a, near_b))
    mix_own, mix_other = kernel(mix_kernel, [table, rows_of(hidden), weight], sums_out(half), values)(
        side, pos, scaled, weight_down
    )
    far_1, core_a, core_b, near_a, near_b, mix_other = together(
        far_1, core_a, core_b, near_a, near_b, mix_other
    )
    with jax.named_scope("over_grads_2"):
        far_2 = over(near_a[1], near_b[1])
    with jax.named_scope("cores_mixed"):
        mix_core = swap_core(mix_other)
        mix_send = sent_first(mix_own, mix_core)
        far_core_1 = cores(far_1)
    far_core_1, mix_send = together(far_core_1, mix_send)
    with jax.named_scope("over_mixed"):
        mix_first = over(*mix_send)
    far_2, mix_send = together(far_2, mix_send)
    with jax.named_scope("cores_grads"):
        far_core_2 = cores(far_2)
    pieces = [
        piece
        for chunk, far, far_core in ((0, far_1, far_core_1), (1, far_2, far_core_2))
        for at, near, core in ((0, near_a, core_a), (1, near_b, core_b))
        for piece in ((near, chunk), (far[at], None), (core, chunk), (far_core[at], None))
    ]
    grad_rows, grad_gate_pre, grad_up_pre, token_sums = kernel(
        back_kernel,
        [table, table] + [piece_of(*piece) for piece in pieces] + [weight, rows_of(hidden), rows_of(hidden)],
        [row_out, hidden_bf, hidden_bf, (shaped((column, 4, tok_count), F32), table)],
    )(side, pos, gate, *(piece for piece, _ in pieces), weight_down, gate_pre, up_pre)

    def input_terms(quarters):
        span = width // 4
        blocks = [
            pl.BlockSpec((hidden, span), lambda i, s, at=4 * far + quarter: (0, at), pipeline_mode=pl.Buffered(1))
            for far in range(2)
            for quarter in quarters
        ]
        count = len(blocks)
        return kernel(
            input_kernel,
            [table, rows_of(hidden), rows_of(hidden)] + blocks * 2,
            sums_out(len(quarters) * span // 2),
            [pltpu.VMEM((step_rows, count * span), BF16)],
        )(side, pos, grad_gate_pre, grad_up_pre, *[weight_gate] * count, *[weight_up] * count)

    own_1, other_1 = input_terms((0, 1, 2))
    own_2, other_2 = input_terms((3,))
    with jax.named_scope("gates"):
        token_sums = token_sums + swap_side(token_sums)
    mix_first, other_1, other_2, token_sums = together(mix_first, other_1, other_2, token_sums)
    with jax.named_scope("across_mixed"):
        mix_send = sent_second(mix_own, mix_core, mix_first)
        mix_second = across(*mix_send)
    with jax.named_scope("cores_inputs"):
        core_1, core_2 = cores((other_1, other_2))
    send_1, send_2 = sent_first(own_1, core_1), sent_first(own_2, core_2)
    scaled, mix_send = together(scaled, mix_send)
    (grad_down,) = weight_grads(grad_rows, scaled)
    send_1, send_2, grad_down = together(send_1, send_2, grad_down)
    with jax.named_scope("over_inputs_1"):
        first_1 = over(*send_1)
    with jax.named_scope("column_mixed"):
        grad_gate_pre, send_1 = together(grad_gate_pre, send_1)
        (grad_gate,) = weight_grads(rows, grad_gate_pre)
        mix_second, grad_gate = together(mix_second, grad_gate)
        mix_both = sent_column(mix_own, mix_core, mix_first, mix_second)
        mix_received = from_column(mix_both)
    grad_up_pre, mix_both = together(grad_up_pre, mix_both)
    (grad_up,) = weight_grads(rows, grad_up_pre)
    first_1, send_2, mix_received[1:], grad_gate, grad_up = together(
        first_1, send_2, mix_received[1:], grad_gate, grad_up
    )
    with jax.named_scope("across_inputs_1"):
        send_1 = sent_second(own_1, core_1, first_1)
        second_1 = across(*send_1)
    with jax.named_scope("over_inputs_2"):
        send_1, send_2 = together(send_1, send_2)
        first_2 = over(*send_2)
    second_1, mix_received = together(second_1, mix_received)
    with jax.named_scope("column_inputs_1"):
        both_1 = sent_column(own_1, core_1, first_1, second_1)
        received_1 = from_column(both_1)
    first_2, both_1 = together(first_2, both_1)
    with jax.named_scope("across_inputs_2"):
        send_2 = sent_second(own_2, core_2, first_2)
        second_2 = across(*send_2)
    mix_received, send_2 = together(mix_received, send_2)
    mixed = column_sum(mix_both[0], mix_received)
    second_2, mixed = together(second_2, mixed)
    with jax.named_scope("column_inputs_2"):
        both_2 = sent_column(own_2, core_2, first_2, second_2)
        received_2 = from_column(both_2)
    token_sums, both_1, both_2 = together(token_sums, both_1, both_2)
    with jax.named_scope("gates"):
        expert_sums = sums_of_experts(token_sums)
    grad_tokens_1 = column_sum(both_1[0], received_1)
    received_2, expert_sums, grad_tokens_1 = together(received_2, expert_sums, grad_tokens_1)
    grad_tokens = jnp.concatenate([grad_tokens_1, column_sum(both_2[0], received_2)], axis=1)

    chosen = expert_ids[None] == jnp.arange(expert_count, dtype=jnp.int32)[:, None, None]
    grad_gates = jnp.sum(jnp.where(chosen, expert_sums[:, :, None], 0.0), axis=0)

    grad_gate, grad_up, grad_down = grad_gate.T[None], grad_up.T[None], grad_down[None]
    return (mixed, grad_tokens, grad_gates, grad_gate, grad_up, grad_down)


def body(tokens, grad_out, gates, expert_ids, w_gate, w_up, w_down):
    expert_count = lax.axis_size("expert")
    tok_count, top_count = expert_ids.shape
    slot_total = tok_count * top_count * 4 // (3 * expert_count) * expert_count
    gathers = expert_count * tok_count <= 2 * slot_total
    shaped = lax.axis_size("tensor") == 2 and expert_count % 4 == 0 and expert_count <= 256
    plan = gather_body if gathers and shaped else slots_body
    return plan(tokens, grad_out, gates, expert_ids, w_gate, w_up, w_down)


def solution(mesh):
    placed = (
        P("expert", "tensor"),
        P("expert", "tensor"),
        P("expert", None),
        P("expert", None),
        P("expert", None, "tensor"),
        P("expert", None, "tensor"),
        P("expert", "tensor", None),
    )
    return jax.shard_map(
        body,
        mesh=mesh,
        in_specs=placed,
        out_specs=(
            P("expert", "tensor"),
            P("expert", "tensor"),
            P("expert", None),
            P("expert", None, "tensor"),
            P("expert", None, "tensor"),
            P("expert", "tensor", None),
        ),
        check_vma=False,
    )
```
